512 devices in a mesh: pair: 8 (over y, z_hi), rng: 64 (over z_lo, x, core).
Axes of the slice: x: 4, y: 4, z: 16 (z_hi: 2, z_lo: 8; z = z_hi * 8 + z_lo), core: 2. Of those that a mesh axis runs over, the one named last changes fastest.
Arguments:
- stack: bfloat16 [8, 2, 16, 163840], P('pair', None, None, 'rng'), as said below
Outputs:
- coherence: float32 [8, 8, 2, 2, 8192], P('pair', None, None, None, 'rng')
Inputs may be any that keep to these rules, and one draw needn't show every extreme that they name: A coherent stack: every date is a scaled and rotated copy of one common scene plus noise of its own.
All inputs are finite; a program needn't handle non-finite values.
Results may differ from the reference program's by a relative error of at most 0.0003.
Values may be sent and summed in bfloat16 or wider, within the bound.
No kernel may reach another device: no remote copies, remote signals or barrier semaphores. Data moves between devices by JAX's collectives and lax.ppermute only.
A program may use at most 64 MiB of HBM per device.

```python
import math
import jax
import jax.numpy as jnp
from jax import lax

ALINES = 16
AZ_TAPS = 31
RG_TAPS = 60
AZ_STEP = 8
RG_STEP = 20
DATES = 8
NR = 163840


def draw_stack(key, part):
    keys = jax.random.split(key, 5)
    scene = jax.random.normal(keys[0], (2, ALINES, NR), jnp.float32)
    noise = jax.random.normal(keys[1], (DATES, 2, ALINES, NR), jnp.float32)
    amplitude = jax.random.uniform(keys[2], (DATES, 1, 1), jnp.float32, 0.4, 1.6)
    theta = jax.random.uniform(keys[3], (DATES, 1, 1), jnp.float32, -math.pi, math.pi)
    spread = jax.random.uniform(keys[4], (DATES, 1, 1), jnp.float32, 0.5, 1.2)
    real_part = amplitude * (scene[0] * jnp.cos(theta) - scene[1] * jnp.sin(theta)) + spread * noise[:, 0]
    imag_part = amplitude * (scene[0] * jnp.sin(theta) + scene[1] * jnp.cos(theta)) + spread * noise[:, 1]
    values = jnp.stack([real_part, imag_part], axis=1)
    return values.astype(jnp.bfloat16)


def setup_inputs(seed: int = 0) -> dict:
    arg_keys = jax.random.split(jax.random.key(seed), 2)
    stack = draw_stack(jax.random.fold_in(arg_keys[1], 71), 0)
    return dict(stack=stack)


epsilon = 1e-06
highest = lax.Precision.HIGHEST

def look_weights():
    lines = jnp.arange(ALINES, dtype=jnp.int32)
    looks = jnp.arange(ALINES // AZ_STEP, dtype=jnp.int32)
    offset = lines[None, :] - (AZ_STEP * looks[:, None] + (AZ_STEP - AZ_TAPS) // 2)
    centred = (offset.astype(jnp.float32) - (AZ_TAPS - 1) / 2.0) / (AZ_TAPS / 4.0)
    inside = (offset >= 0) & (offset < AZ_TAPS)
    az_weights = jnp.where(inside, jnp.exp(-0.5 * centred * centred), jnp.zeros_like(centred))
    taps = jnp.arange(RG_TAPS, dtype=jnp.int32).astype(jnp.float32)
    centred_range = (taps - (RG_TAPS - 1) / 2.0) / (RG_TAPS / 4.0)
    range_weights = jnp.exp(-0.5 * centred_range * centred_range).reshape(3, RG_STEP)
    return (az_weights, range_weights)

def multilook(product, az_weights, range_weights):
    columns = product.shape[-1] // RG_STEP - 2
    blocks = product.reshape(product.shape[:-1] + (columns + 2, RG_STEP))
    summed = jnp.einsum('...lrc,c->...lr', blocks[..., 0:columns, :], range_weights[0], precision=highest)
    summed = summed + jnp.einsum('...lrc,c->...lr', blocks[..., 1:columns + 1, :], range_weights[1], precision=highest)
    summed = summed + jnp.einsum('...lrc,c->...lr', blocks[..., 2:columns + 2, :], range_weights[2], precision=highest)
    return jnp.einsum('al,...lr->...ar', az_weights, summed, precision=highest)

def reference(stack):
    az_weights, range_weights = look_weights()
    padded = jnp.pad(stack, ((0, 0), (0, 0), (0, 0), (RG_STEP, RG_STEP)))

    def power_of(tile):
        values = tile.astype(jnp.float32)
        return multilook(values[0] * values[0] + values[1] * values[1], az_weights, range_weights)
    powers = lax.map(power_of, padded) + epsilon

    def row_of(index):
        row_tile = lax.dynamic_index_in_dim(padded, index, 0, keepdims=False).astype(jnp.float32)
        row_power = lax.dynamic_index_in_dim(powers, index, 0, keepdims=False)

        def entry(column):
            col_tile = lax.dynamic_index_in_dim(padded, column, 0, keepdims=False).astype(jnp.float32)
            col_power = lax.dynamic_index_in_dim(powers, column, 0, keepdims=False)
            real_part = row_tile[0] * col_tile[0] + row_tile[1] * col_tile[1]
            imag_part = row_tile[1] * col_tile[0] - row_tile[0] * col_tile[1]
            cross = multilook(jnp.stack([real_part, imag_part]), az_weights, range_weights)
            return cross * lax.rsqrt(row_power * col_power)[None]
        return lax.map(entry, jnp.arange(DATES, dtype=jnp.int32))
    return lax.map(row_of, jnp.arange(DATES, dtype=jnp.int32))
```

```python
import math

import jax
import jax.numpy as jnp
from jax import lax
from jax.experimental import pallas as pl
from jax.experimental.pallas import tpu as pltpu
from jax.sharding import PartitionSpec as P

AZ_TAPS = 31
RG_TAPS = 60
AZ_STEP = 8
RG_STEP = 20
LINES = 16
LANES = 128
EPSILON = 1e-06

Y = 4
GROUPS = [[0, 2, 4, 6], [1, 3, 5, 7]]
INNER = [(i, j) for i in range(Y) for j in range(i + 1, Y)]

f32 = jnp.float32
bf16 = jnp.bfloat16
VMEM = pl.BlockSpec(memory_space=pltpu.VMEM)


def place():
    pair = lax.axis_index("pair")
    return pair // 2, pair % 2


def azimuth_weights():
    line = lax.broadcasted_iota(jnp.int32, (LINES, LANES), 0)
    weights = []
    for look in range(LINES // AZ_STEP):
        offset = line - (AZ_STEP * look + (AZ_STEP - AZ_TAPS) // 2)
        centred = (offset.astype(f32) - (AZ_TAPS - 1) / 2.0) / (AZ_TAPS / 4.0)
        inside = (offset >= 0) & (offset < AZ_TAPS)
        weights.append(jnp.where(inside, jnp.exp(-0.5 * centred * centred), 0.0))
    return weights


def range_weights(quarter, rows, columns):
    row = lax.broadcasted_iota(jnp.int32, (rows + LANES, columns), 0)
    look = lax.broadcasted_iota(jnp.int32, (rows + LANES, columns), 1)
    own = quarter * rows + row
    halo = row - rows + jnp.where(quarter == 0, -LANES, Y * rows)
    sample = jnp.where(row < rows, own, halo)
    tap = sample - RG_STEP * (look - 1)
    centred = (tap.astype(f32) - (RG_TAPS - 1) / 2.0) / (RG_TAPS / 4.0)
    inside = (tap >= 0) & (tap < RG_TAPS)
    return jnp.where(inside, 2.0 * jnp.exp(-0.5 * centred * centred), 0.0)


def prepare_kernel(group_ref, edge_ref, weight_ref):
    quarter, _ = place()
    width = group_ref.shape[-1]
    first = group_ref[:, :, :, 0:LANES]
    last = group_ref[:, :, :, width - LANES : width]
    edge_ref[...] = jnp.where(quarter == Y - 1, last, first)
    weights = range_weights(quarter, width, LANES)
    high = weights.astype(bf16)
    weight_ref[:, 0:LANES] = high
    weight_ref[:, LANES : 2 * LANES] = (weights - high.astype(f32)).astype(bf16)


def load(ref, halo_ref, date, at):
    width = ref.shape[-1]
    if at < width:
        tile = ref[date, :, :, at : at + LANES]
    else:
        tile = halo_ref[date]
    tile = tile.astype(f32)
    return tile[0], tile[1]


def put(x_ref, fields, field, at, value):
    high = value.astype(bf16)
    low = (value - high.astype(f32)).astype(bf16)
    x_ref[field * LINES : (field + 1) * LINES, at : at + LANES] = high
    x_ref[(fields + field) * LINES : (fields + field + 1) * LINES, at : at + LANES] = low


def looks_of(x_ref, weight_ref, d_ref, fields):
    d_ref[...] = jnp.dot(x_ref[...], weight_ref[...], preferred_element_type=f32)
    weights = azimuth_weights()
    for field in range(fields):
        high = d_ref[field * LINES : (field + 1) * LINES, :]
        low = d_ref[(fields + field) * LINES : (fields + field + 1) * LINES, :]
        both = high + low
        summed = both[:, 0:LANES] + both[:, LANES : 2 * LANES]
        yield field, [jnp.sum(summed * w, axis=0, keepdims=True) for w in weights]


def inner_kernel(group_ref, halo_ref, weight_ref, out_ref, x_ref, d_ref):
    fields = Y + 2 * len(INNER)
    for at in range(0, group_ref.shape[-1] + LANES, LANES):
        dates = [load(group_ref, halo_ref, i, at) for i in range(Y)]
        halves = [(0.5 * x, 0.5 * y) for x, y in dates]
        for i, ((x, y), (hx, hy)) in enumerate(zip(dates, halves)):
            put(x_ref, fields, i, at, hx * x + hy * y)
        for k, (i, j) in enumerate(INNER):
            (hx, hy), (x, y) = halves[i], dates[j]
            put(x_ref, fields, Y + 2 * k, at, hx * x + hy * y)
            put(x_ref, fields, Y + 2 * k + 1, at, hy * x - hx * y)
    for field, rows in looks_of(x_ref, weight_ref, d_ref, fields):
        for a, row in enumerate(rows):
            out_ref[2 * field + a : 2 * field + a + 1, :] = row


def outer_kernel(group_ref, other_ref, group_halo_ref, other_halo_ref, weight_ref, inner_ref, out_ref, x_ref, d_ref):
    _, here = place()
    there = 1 - here
    fields = Y + 2 * Y * Y
    for at in range(0, group_ref.shape[-1] + LANES, LANES):
        dates = [load(other_ref, other_halo_ref, j, at) for j in range(Y)]
        for j, (x, y) in enumerate(dates):
            put(x_ref, fields, j, at, (0.5 * x) * x + (0.5 * y) * y)
        for i in range(Y):
            x, y = load(group_ref, group_halo_ref, i, at)
            hx, hy = 0.5 * x, 0.5 * y
            for j, (x, y) in enumerate(dates):
                field = Y + 2 * (Y * i + j)
                put(x_ref, fields, field, at, hx * x + hy * y)
                put(x_ref, fields, field + 1, at, hy * x - hx * y)

    def store(i, side, part, j, a, row):
        at = 8 * part + 2 * j + a
        out_ref[i, side, at : at + 1, :] = row

    def inner(field, a):
        return inner_ref[2 * field + a : 2 * field + a + 1, :]

    for a in range(2):
        for j in range(Y):
            power = inner(j, a)
            store(j, here, 0, j, a, power)
            store(j, here, 1, j, a, jnp.zeros_like(power))
            for i in range(Y):
                store(i, here, 2, j, a, power)
                store(j, here, 3, i, a, power)
                store(j, there, 3, i, a, power)
        for k, (i, j) in enumerate(INNER):
            real, imag = inner(Y + 2 * k, a), inner(Y + 2 * k + 1, a)
            store(i, here, 0, j, a, real)
            store(i, here, 1, j, a, imag)
            store(j, here, 0, i, a, real)
            store(j, here, 1, i, a, -imag)
    for field, rows in looks_of(x_ref, weight_ref, d_ref, fields):
        for a, row in enumerate(rows):
            if field < Y:
                for i in range(Y):
                    store(i, there, 2, field, a, row)
            else:
                i, j = divmod((field - Y) // 2, Y)
                store(i, there, (field - Y) % 2, j, a, row)


def normalise_kernel(parts_ref, out_ref):
    for side in range(2):
        summed = parts_ref[0, side] + parts_ref[1, side] + parts_ref[2, side] + parts_ref[3, side]
        scale = lax.rsqrt((summed[24:32] + EPSILON) * (summed[16:24] + EPSILON))
        for k in range(2):
            rows = summed[8 * k : 8 * k + 8] * scale
            for j in range(Y):
                out_ref[2 * j + side, k] = rows[2 * j : 2 * j + 2]


def call(kernel, out_shape, operands, scratch=(), cost=0):
    return pl.pallas_call(
        kernel,
        out_shape=out_shape,
        in_specs=[VMEM] * len(operands),
        out_specs=jax.tree.map(lambda _: VMEM, out_shape),
        scratch_shapes=list(scratch),
        cost_estimate=pl.CostEstimate(flops=cost, bytes_accessed=1 << 20, transcendentals=0),
    )(*operands)


def edges(tiles, swap):
    pairs = []
    for h in range(2):
        for n in range(tiles):
            source = (h ^ swap) * tiles + n
            if n + 1 < tiles:
                pairs.append((2 * (Y - 1) * tiles + source, h * tiles + n + 1))
            if n > 0:
                pairs.append((source, (2 * (Y - 1) + h) * tiles + n - 1))
    return pairs


def local(stack):
    tiles = lax.axis_size("rng")
    width = stack.shape[-1] // Y
    axes = ("pair", "rng")
    across = [((2 * y + h) * tiles + n, (2 * y + 1 - h) * tiles + n) for y in range(Y) for h in range(2) for n in range(tiles)]

    chunks = stack[0].reshape(2, LINES, Y, width).transpose(2, 0, 1, 3)
    group = lax.all_to_all(chunks, "pair", 0, 0, axis_index_groups=GROUPS)
    other = lax.ppermute(group, axes, across)

    depth = width + LANES
    edge, weights = call(
        prepare_kernel,
        (jax.ShapeDtypeStruct((Y, 2, LINES, LANES), bf16), jax.ShapeDtypeStruct((depth, 2 * LANES), bf16)),
        (group,),
        cost=10 * depth * LANES,
    )
    other_halo = lax.ppermute(edge, axes, edges(tiles, 1))
    group_halo = lax.ppermute(edge, axes, edges(tiles, 0))

    def scratch(fields):
        return [pltpu.VMEM((2 * fields * LINES, depth), bf16), pltpu.VMEM((2 * fields * LINES, 2 * LANES), f32)]

    fields = Y + 2 * len(INNER)
    inner = call(
        inner_kernel,
        jax.ShapeDtypeStruct((2 * fields, LANES), f32),
        (group, group_halo, weights),
        scratch(fields),
        cost=2 * 2 * fields * LINES * depth * 2 * LANES,
    )
    fields = Y + 2 * Y * Y
    parts = call(
        outer_kernel,
        jax.ShapeDtypeStruct((Y, 2, 32, LANES), f32),
        (group, other, group_halo, other_halo, weights, inner),
        scratch(fields),
        cost=2 * 2 * fields * LINES * depth * 2 * LANES,
    )
    parts = lax.all_to_all(parts, "pair", 0, 0, axis_index_groups=GROUPS)
    out = call(normalise_kernel, jax.ShapeDtypeStruct((2 * Y, 2, 2, LANES), f32), (parts,))
    return out[None]


def solution(mesh):
    in_specs = (P("pair", None, None, "rng"),)
    out_specs = P("pair", None, None, None, "rng")
    return jax.shard_map(local, mesh=mesh, in_specs=in_specs, out_specs=out_specs, check_vma=False)
```

```python
import jax
import jax.numpy as jnp
from jax import lax
from jax.experimental import pallas as pl
from jax.experimental.pallas import tpu as pltpu
from jax.sharding import PartitionSpec as P

AZ_TAPS = 31
RG_TAPS = 60
AZ_STEP = 8
RG_STEP = 20
LINES = 16
LANES = 128
SLOT = 32
EPSILON = 1e-06
VMEM_LIMIT = 8 << 20

Y = 4
GROUPS = [[0, 2, 4, 6], [1, 3, 5, 7]]
INNER = [(i, j) for i in range(Y) for j in range(i + 1, Y)]
N_INNER = Y + 2 * len(INNER)
N_OUTER = Y + 2 * Y * Y

f32 = jnp.float32
bf16 = jnp.bfloat16
VMEM = pl.BlockSpec(memory_space=pltpu.VMEM)


def quarter_of(y):
    return jnp.where(lax.axis_index("rng") % 2 == 1, Y - 1 - y, y)


def here():
    pair = lax.axis_index("pair")
    return quarter_of(pair // 2), pair % 2


def lanes(rows):
    return lax.broadcasted_iota(jnp.int32, (rows, LANES), 1)


def azimuth_weights():
    line = lax.broadcasted_iota(jnp.int32, (LINES, LANES), 0)
    weights = []
    for look in range(LINES // AZ_STEP):
        offset = line - (AZ_STEP * look + (AZ_STEP - AZ_TAPS) // 2)
        centred = (offset.astype(f32) - (AZ_TAPS - 1) / 2.0) / (AZ_TAPS / 4.0)
        inside = (offset >= 0) & (offset < AZ_TAPS)
        weights.append(jnp.where(inside, jnp.exp(-0.5 * centred * centred), 0.0))
    return weights


def range_weights(quarter, width):
    shape = (width + LANES, LANES)
    row = lax.broadcasted_iota(jnp.int32, shape, 0)
    look = lax.broadcasted_iota(jnp.int32, shape, 1)
    halo = row - width + jnp.where(quarter == 0, -RG_STEP, Y * width)
    sample = jnp.where(row < width, quarter * width + row, halo)
    tap = sample - RG_STEP * (look - 1)
    centred = (tap.astype(f32) - (RG_TAPS - 1) / 2.0) / (RG_TAPS / 4.0)
    inside = (tap >= 0) & (tap < RG_TAPS) & (row < width + RG_STEP)
    return jnp.where(inside, 2.0 * jnp.exp(-0.5 * centred * centred), 0.0)


def cut_kernel(stack_ref, out_ref):
    blocks = out_ref.shape[2]
    for q in range(Y):
        to = quarter_of(q)
        for part in range(2):
            for t in range(blocks):
                at = (q * blocks + t) * LANES
                out_ref[to, part, t] = stack_ref[0, part, :, at : at + LANES]


def edge_kernel(group_ref, edge_ref):
    quarter, _ = here()
    blocks = group_ref.shape[2]
    for part in range(2):
        packed = jnp.zeros((LINES, LANES), f32)
        for i in range(Y):
            first = group_ref[i, part, 0].astype(f32)
            last = group_ref[i, part, blocks - 1].astype(f32)
            edge = jnp.where(quarter == Y - 1, pltpu.roll(last, RG_STEP, 1), first)
            edge = jnp.where(lanes(LINES) < RG_STEP, edge, 0.0)
            packed = packed + (pltpu.roll(edge, SLOT * i, 1) if i else edge)
        edge_ref[part] = packed.astype(bf16)


def join_kernel(group_ref, halo_ref, out_ref):
    blocks = group_ref.shape[2]
    for i in range(Y):
        for part in range(2):
            for t in range(blocks):
                out_ref[(2 * i + part) * blocks + t] = group_ref[i, part, t]
    for part in range(2):
        out_ref[2 * Y * blocks + part] = halo_ref[part]


def blocks_of(ref):
    return (ref.shape[0] - 2) // (2 * Y)


def dates_at(ref, t):
    blocks = blocks_of(ref)
    if t < blocks:
        return [tuple(ref[(2 * i + part) * blocks + t].astype(f32) for part in range(2)) for i in range(Y)]
    packed = [ref[2 * Y * blocks + part].astype(f32) for part in range(2)]
    inside = lanes(LINES) < RG_STEP
    rolled = [[pltpu.roll(p, LANES - SLOT * i, 1) if i else p for p in packed] for i in range(Y)]
    return [tuple(jnp.where(inside, p, 0.0) for p in date) for date in rolled]


def power(date):
    x, y = date
    return ((0.5 * x) * x + (0.5 * y) * y,)


def cross(row, column):
    hx, hy = 0.5 * row[0], 0.5 * row[1]
    x, y = column
    return hx * x + hy * y, hy * x - hx * y


def put(x_ref, fields, t, values):
    at = t * LANES
    for field, value in enumerate(values):
        high = value.astype(bf16)
        low = (value - high.astype(f32)).astype(bf16)
        x_ref[field * LINES : (field + 1) * LINES, at : at + LANES] = high
        x_ref[(fields + field) * LINES : (fields + field + 1) * LINES, at : at + LANES] = low


def looks_of(x_ref, weights, d_ref, fields):
    d_ref[...] = jnp.dot(x_ref[...], weights, preferred_element_type=f32)
    azimuth = azimuth_weights()
    for field in range(fields):
        high = d_ref[field * LINES : (field + 1) * LINES, :]
        low = d_ref[(fields + field) * LINES : (fields + field + 1) * LINES, :]
        both = high + low
        summed = both[:, 0:LANES] + both[:, LANES : 2 * LANES]
        for a, weight in enumerate(azimuth):
            yield field, a, jnp.sum(summed * weight, axis=0, keepdims=True)


def inner_kernel(group_ref, out_ref, weight_ref, x_ref, d_ref):
    blocks = blocks_of(group_ref)
    quarter, _ = here()
    weights = range_weights(quarter, blocks * LANES)
    high = weights.astype(bf16)
    weight_ref[:, 0:LANES] = high
    weight_ref[:, LANES : 2 * LANES] = (weights - high.astype(f32)).astype(bf16)
    for t in range(blocks + 1):
        group = dates_at(group_ref, t)
        fields = [power(d) for d in group] + [cross(group[i], group[j]) for i, j in INNER]
        put(x_ref, N_INNER, t, [value for field in fields for value in field])
    for field, a, row in looks_of(x_ref, weight_ref[...], d_ref, N_INNER):
        out_ref[2 * field + a : 2 * field + a + 1, :] = row


def outer_kernel(group_ref, other_ref, weight_ref, inner_ref, out_ref, x_ref, d_ref):
    _, own = here()
    across = 1 - own
    for t in range(blocks_of(group_ref) + 1):
        group, other = dates_at(group_ref, t), dates_at(other_ref, t)
        fields = [power(d) for d in other] + [cross(i, j) for i in group for j in other]
        put(x_ref, N_OUTER, t, [value for field in fields for value in field])

    def store(i, side, part, j, a, row):
        at = 8 * part + 2 * j + a
        out_ref[i, side, at : at + 1, :] = row

    def inner(field, a):
        return inner_ref[2 * field + a : 2 * field + a + 1, :]

    for a in range(2):
        for j in range(Y):
            row = inner(j, a)
            store(j, own, 0, j, a, row)
            store(j, own, 1, j, a, jnp.zeros_like(row))
            for i in range(Y):
                store(i, own, 2, j, a, row)
                store(j, own, 3, i, a, row)
                store(j, across, 3, i, a, row)
        for k, (i, j) in enumerate(INNER):
            real, imag = inner(Y + 2 * k, a), inner(Y + 2 * k + 1, a)
            store(i, own, 0, j, a, real)
            store(i, own, 1, j, a, imag)
            store(j, own, 0, i, a, real)
            store(j, own, 1, i, a, -imag)
    for field, a, row in looks_of(x_ref, weight_ref[...], d_ref, N_OUTER):
        if field < Y:
            for i in range(Y):
                store(i, across, 2, field, a, row)
        else:
            i, j = divmod((field - Y) // 2, Y)
            store(i, across, (field - Y) % 2, j, a, row)


def normalise_kernel(parts_ref, out_ref):
    for side in range(2):
        summed = parts_ref[0, side] + parts_ref[1, side] + parts_ref[2, side] + parts_ref[3, side]
        scale = lax.rsqrt((summed[24:32] + EPSILON) * (summed[16:24] + EPSILON))
        for k in range(2):
            rows = summed[8 * k : 8 * k + 8] * scale
            for j in range(Y):
                out_ref[2 * j + side, k] = rows[2 * j : 2 * j + 2]


def call(kernel, out_shape, operands, scratch=(), flops=0):
    return pl.pallas_call(
        kernel,
        out_shape=out_shape,
        in_specs=[VMEM] * len(operands),
        out_specs=jax.tree.map(lambda _: VMEM, out_shape),
        scratch_shapes=list(scratch),
        compiler_params=pltpu.CompilerParams(vmem_limit_bytes=VMEM_LIMIT),
        cost_estimate=pl.CostEstimate(flops=flops, bytes_accessed=1 << 20, transcendentals=0),
    )(*operands)


def looks(kernel, out_shape, operands, fields, samples):
    rows = 2 * fields * LINES
    scratch = [pltpu.VMEM((rows, samples), bf16), pltpu.VMEM((rows, 2 * LANES), f32)]
    return call(kernel, out_shape, operands, scratch, flops=2 * rows * samples * 2 * LANES)


def local(stack):
    tiles = lax.axis_size("rng")
    blocks = stack.shape[-1] // (Y * LANES)
    axes = ("pair", "rng")

    def device(y, h, n):
        return (2 * y + h) * tiles + n

    across = [(device(y, h, n), device(y, 1 - h, n)) for y in range(Y) for h in range(2) for n in range(tiles)]
    swap = []
    for h in range(2):
        for n in range(tiles - 1):
            y = 0 if n % 2 else Y - 1
            swap += [(device(y, h, n), device(y, h, n + 1)), (device(y, h, n + 1), device(y, h, n))]

    chunks = call(cut_kernel, jax.ShapeDtypeStruct((Y, 2, blocks, LINES, LANES), bf16), (stack,))
    group = lax.all_to_all(chunks, "pair", 0, 0, axis_index_groups=GROUPS)
    edge = call(edge_kernel, jax.ShapeDtypeStruct((2, LINES, LANES), bf16), (group,))
    halo = lax.ppermute(edge, axes, swap)
    group = call(join_kernel, jax.ShapeDtypeStruct((2 * Y * blocks + 2, LINES, LANES), bf16), (group, halo))
    other = lax.ppermute(group, axes, across)

    samples = (blocks + 1) * LANES
    inner, weights = looks(
        inner_kernel,
        (jax.ShapeDtypeStruct((2 * N_INNER, LANES), f32), jax.ShapeDtypeStruct((samples, 2 * LANES), bf16)),
        (group,),
        N_INNER,
        samples,
    )
    parts = looks(
        outer_kernel,
        jax.ShapeDtypeStruct((Y, 2, 32, LANES), f32),
        (group, other, weights, inner),
        N_OUTER,
        samples,
    )
    parts = lax.all_to_all(parts, "pair", 0, 0, axis_index_groups=GROUPS)
    out = call(normalise_kernel, jax.ShapeDtypeStruct((2 * Y, 2, 2, LANES), f32), (parts,))
    return out[None]


def solution(mesh):
    in_specs = (P("pair", None, None, "rng"),)
    out_specs = P("pair", None, None, None, "rng")
    return jax.shard_map(local, mesh=mesh, in_specs=in_specs, out_specs=out_specs, check_vma=False)
```

```python
import jax
import jax.numpy as jnp
from jax import lax
from jax.experimental import pallas as pl
from jax.experimental.pallas import tpu as pltpu
from jax.sharding import PartitionSpec as P

AZ_TAPS = 31
RG_TAPS = 60
AZ_STEP = 8
RG_STEP = 20
LINES = 16
LANES = 128
SLOT = 32
EPSILON = 1e-06
VMEM_LIMIT = 8 << 20

Y = 4
GROUPS = [[0, 2, 4, 6], [1, 3, 5, 7]]
INNER = [(i, j) for i in range(Y) for j in range(i + 1, Y)]
SHARES = (3, 6, 6, 5)
BLOCKS = max(SHARES)
EDGES = (0, Y - 1)
N_INNER = Y + 2 * len(INNER)
N_OUTER = Y + 2 * Y * Y

f32 = jnp.float32
bf16 = jnp.bfloat16
VMEM = pl.BlockSpec(memory_space=pltpu.VMEM)


def place():
    pair = lax.axis_index("pair")
    return pair // 2, pair % 2, lax.axis_index("rng") % 2 == 1


def start_of(y, odd):
    return jnp.where(odd, sum(SHARES[y + 1 :]), sum(SHARES[:y]))


def pick(y, values):
    out = jnp.int32(values[0])
    for i in range(1, Y):
        out = jnp.where(y == i, values[i], out)
    return out


def at_left(y, odd):
    return (y == 0) != odd


def lanes(rows):
    return lax.broadcasted_iota(jnp.int32, (rows, LANES), 1)


def azimuth_weights():
    line = lax.broadcasted_iota(jnp.int32, (LINES, LANES), 0)
    weights = []
    for look in range(LINES // AZ_STEP):
        offset = line - (AZ_STEP * look + (AZ_STEP - AZ_TAPS) // 2)
        centred = (offset.astype(f32) - (AZ_TAPS - 1) / 2.0) / (AZ_TAPS / 4.0)
        inside = (offset >= 0) & (offset < AZ_TAPS)
        weights.append(jnp.where(inside, jnp.exp(-0.5 * centred * centred), 0.0))
    return weights


def range_weights(y, odd):
    shape = (BLOCKS * LANES, LANES)
    row = lax.broadcasted_iota(jnp.int32, shape, 0)
    look = lax.broadcasted_iota(jnp.int32, shape, 1)
    start = jnp.where(odd, pick(y, [sum(SHARES[i + 1 :]) for i in range(Y)]), pick(y, [sum(SHARES[:i]) for i in range(Y)]))
    count = pick(y, SHARES) * LANES
    halo = row - (BLOCKS - 1) * LANES
    beyond = halo + jnp.where(at_left(y, odd), -RG_STEP, sum(SHARES) * LANES)
    own = row < count
    sample = jnp.where(own, start * LANES + row, beyond)
    tap = sample - RG_STEP * (look - 1)
    centred = (tap.astype(f32) - (RG_TAPS - 1) / 2.0) / (RG_TAPS / 4.0)
    inside = (tap >= 0) & (tap < RG_TAPS) & (own | ((halo >= 0) & (halo < RG_STEP)))
    return jnp.where(inside, 2.0 * jnp.exp(-0.5 * centred * centred), 0.0)


def cut_kernel(stack_ref, out_ref):
    _, _, odd = place()
    for y in range(Y):
        start = start_of(y, odd)
        for part in range(2):
            for t in range(BLOCKS):
                if t < SHARES[y]:
                    at = pl.multiple_of((start + t) * LANES, LANES)
                    out_ref[y, part, t] = stack_ref[0, part, :, pl.ds(at, LANES)]
                else:
                    out_ref[y, part, t] = jnp.zeros((LINES, LANES), bf16)


def edge_kernel(group_ref, edge_ref):
    y, _, odd = place()
    for part in range(2):
        packed = jnp.zeros((LINES, LANES), f32)
        for i in range(Y):
            first = group_ref[i, part, 0].astype(f32)
            last = jnp.where(y == 0, group_ref[i, part, SHARES[0] - 1], group_ref[i, part, SHARES[Y - 1] - 1]).astype(f32)
            edge = jnp.where(at_left(y, odd), first, pltpu.roll(last, RG_STEP, 1))
            edge = jnp.where(lanes(LINES) < RG_STEP, edge, 0.0)
            packed = packed + (pltpu.roll(edge, SLOT * i, 1) if i else edge)
        edge_ref[part] = packed.astype(bf16)


def join_kernel(group_ref, halo_ref, *out_refs):
    for out_ref, y in zip(out_refs, EDGES):
        share = SHARES[y]
        for i in range(Y):
            for part in range(2):
                for t in range(share):
                    out_ref[(2 * i + part) * share + t] = group_ref[i, part, t]
        for part in range(2):
            out_ref[2 * Y * share + part] = halo_ref[part]


def unpack(packed, i):
    rolled = pltpu.roll(packed, LANES - SLOT * i, 1) if i else packed
    return jnp.where(lanes(LINES) < RG_STEP, rolled, 0.0)


def dates_at(ref, t, halos, joined=()):
    def one(i, part):
        value = ref[i, part, t].astype(f32)
        for joined_ref, y in joined:
            if t < SHARES[y]:
                value = value + joined_ref[(2 * i + part) * SHARES[y] + t].astype(f32)
        if t == BLOCKS - 1:
            value = value + unpack(halos[part], i)
        return value

    return [(one(i, 0), one(i, 1)) for i in range(Y)]


def power(date):
    x, y = date
    return ((0.5 * x) * x + (0.5 * y) * y,)


def cross(row, column):
    hx, hy = 0.5 * row[0], 0.5 * row[1]
    x, y = column
    return hx * x + hy * y, hy * x - hx * y


def put(x_ref, fields, t, values):
    at = t * LANES
    for field, value in enumerate(values):
        high = value.astype(bf16)
        low = (value - high.astype(f32)).astype(bf16)
        x_ref[field * LINES : (field + 1) * LINES, at : at + LANES] = high
        x_ref[(fields + field) * LINES : (fields + field + 1) * LINES, at : at + LANES] = low


def looks_of(x_ref, weights, d_ref, fields):
    d_ref[...] = jnp.dot(x_ref[...], weights, preferred_element_type=f32)
    azimuth = azimuth_weights()
    for field in range(fields):
        high = d_ref[field * LINES : (field + 1) * LINES, :]
        low = d_ref[(fields + field) * LINES : (fields + field + 1) * LINES, :]
        both = high + low
        summed = both[:, 0:LANES] + both[:, LANES : 2 * LANES]
        for a, weight in enumerate(azimuth):
            yield field, a, jnp.sum(summed * weight, axis=0, keepdims=True)


def inner_kernel(group_ref, halo_ref, out_ref, weight_ref, x_ref, d_ref):
    y, _, odd = place()
    weights = range_weights(y, odd)
    high = weights.astype(bf16)
    weight_ref[:, 0:LANES] = high
    weight_ref[:, LANES : 2 * LANES] = (weights - high.astype(f32)).astype(bf16)
    halos = [halo_ref[part].astype(f32) for part in range(2)]
    for t in range(BLOCKS):
        group = dates_at(group_ref, t, halos)
        fields = [power(d) for d in group] + [cross(group[i], group[j]) for i, j in INNER]
        put(x_ref, N_INNER, t, [value for field in fields for value in field])
    for field, a, row in looks_of(x_ref, weight_ref[...], d_ref, N_INNER):
        out_ref[2 * field + a : 2 * field + a + 1, :] = row


def outer_kernel(group_ref, halo_ref, other_ref, first_ref, last_ref, weight_ref, inner_ref, out_ref, x_ref, d_ref):
    _, own, _ = place()
    across = 1 - own
    halos = [halo_ref[part].astype(f32) for part in range(2)]
    joined = list(zip((first_ref, last_ref), EDGES))
    other_halos = [sum(ref[2 * Y * SHARES[y] + part].astype(f32) for ref, y in joined) for part in range(2)]
    for t in range(BLOCKS):
        group, other = dates_at(group_ref, t, halos), dates_at(other_ref, t, other_halos, joined)
        fields = [power(d) for d in other] + [cross(i, j) for i in group for j in other]
        put(x_ref, N_OUTER, t, [value for field in fields for value in field])

    def store(i, side, part, j, a, row):
        at = 8 * part + 2 * j + a
        out_ref[i, side, at : at + 1, :] = row

    def inner(field, a):
        return inner_ref[2 * field + a : 2 * field + a + 1, :]

    for a in range(2):
        for j in range(Y):
            row = inner(j, a)
            store(j, own, 0, j, a, row)
            store(j, own, 1, j, a, jnp.zeros_like(row))
            for i in range(Y):
                store(i, own, 2, j, a, row)
                store(j, own, 3, i, a, row)
                store(j, across, 3, i, a, row)
        for k, (i, j) in enumerate(INNER):
            real, imag = inner(Y + 2 * k, a), inner(Y + 2 * k + 1, a)
            store(i, own, 0, j, a, real)
            store(i, own, 1, j, a, imag)
            store(j, own, 0, i, a, real)
            store(j, own, 1, i, a, -imag)
    for field, a, row in looks_of(x_ref, weight_ref[...], d_ref, N_OUTER):
        if field < Y:
            for i in range(Y):
                store(i, across, 2, field, a, row)
        else:
            i, j = divmod((field - Y) // 2, Y)
            store(i, across, (field - Y) % 2, j, a, row)


def normalise_kernel(parts_ref, out_ref):
    for side in range(2):
        summed = parts_ref[0, side] + parts_ref[1, side] + parts_ref[2, side] + parts_ref[3, side]
        scale = lax.rsqrt((summed[24:32] + EPSILON) * (summed[16:24] + EPSILON))
        for k in range(2):
            rows = summed[8 * k : 8 * k + 8] * scale
            for j in range(Y):
                out_ref[2 * j + side, k] = rows[2 * j : 2 * j + 2]


def call(kernel, out_shape, operands, scratch=(), flops=0):
    return pl.pallas_call(
        kernel,
        out_shape=out_shape,
        in_specs=[VMEM] * len(operands),
        out_specs=jax.tree.map(lambda _: VMEM, out_shape),
        scratch_shapes=list(scratch),
        compiler_params=pltpu.CompilerParams(vmem_limit_bytes=VMEM_LIMIT),
        cost_estimate=pl.CostEstimate(flops=flops, bytes_accessed=1 << 20, transcendentals=0),
    )(*operands)


def looks(kernel, out_shape, operands, fields):
    rows, samples = 2 * fields * LINES, BLOCKS * LANES
    scratch = [pltpu.VMEM((rows, samples), bf16), pltpu.VMEM((rows, 2 * LANES), f32)]
    return call(kernel, out_shape, operands, scratch, flops=2 * rows * samples * 2 * LANES)


def local(stack):
    tiles = lax.axis_size("rng")
    axes = ("pair", "rng")

    def device(y, h, n):
        return (2 * y + h) * tiles + n

    def across(*ys):
        return [(device(y, h, n), device(y, 1 - h, n)) for y in ys for h in range(2) for n in range(tiles)]

    swap = []
    for h in range(2):
        for n in range(tiles - 1):
            y = EDGES[(n + 1) % 2]
            swap += [(device(y, h, n), device(y, h, n + 1)), (device(y, h, n + 1), device(y, h, n))]

    chunks = call(cut_kernel, jax.ShapeDtypeStruct((Y, 2, BLOCKS, LINES, LANES), bf16), (stack,))
    group = lax.all_to_all(chunks, "pair", 0, 0, axis_index_groups=GROUPS)
    other = lax.ppermute(group, axes, across(1, 2))
    edge = call(edge_kernel, jax.ShapeDtypeStruct((2, LINES, LANES), bf16), (group,))
    halo = lax.ppermute(edge, axes, swap)
    shapes = tuple(jax.ShapeDtypeStruct((2 * Y * SHARES[y] + 2, LINES, LANES), bf16) for y in EDGES)
    first, last = call(join_kernel, shapes, (group, halo))
    first = lax.ppermute(first, axes, across(0))
    last = lax.ppermute(last, axes, across(Y - 1))

    shapes = (
        jax.ShapeDtypeStruct((2 * N_INNER, LANES), f32),
        jax.ShapeDtypeStruct((BLOCKS * LANES, 2 * LANES), bf16),
    )
    inner, weights = looks(inner_kernel, shapes, (group, halo), N_INNER)
    parts = looks(
        outer_kernel,
        jax.ShapeDtypeStruct((Y, 2, 32, LANES), f32),
        (group, halo, other, first, last, weights, inner),
        N_OUTER,
    )
    parts = lax.all_to_all(parts, "pair", 0, 0, axis_index_groups=GROUPS)
    out = call(normalise_kernel, jax.ShapeDtypeStruct((2 * Y, 2, 2, LANES), f32), (parts,))
    return out[None]


def solution(mesh):
    in_specs = (P("pair", None, None, "rng"),)
    out_specs = P("pair", None, None, None, "rng")
    return jax.shard_map(local, mesh=mesh, in_specs=in_specs, out_specs=out_specs, check_vma=False)
```

```python
import jax
import jax.numpy as jnp
from jax import lax
from jax.experimental import pallas as pl
from jax.experimental.pallas import tpu as pltpu
from jax.sharding import PartitionSpec as P

AZ_TAPS = 31
RG_TAPS = 60
AZ_STEP = 8
RG_STEP = 20
LINES = 16
LANES = 128
SLOT = 32
WINDOW = 64
EPSILON = 1e-06
VMEM_LIMIT = 8 << 20

Y = 4
GROUPS = [[0, 2, 4, 6], [1, 3, 5, 7]]
INNER = [(i, j) for i in range(Y) for j in range(i + 1, Y)]
SHARES = (2, 6, 6, 6)
BLOCKS = max(SHARES)
LOOKS = sum(SHARES) * LANES // RG_STEP
N_INNER = Y + 2 * len(INNER)
N_OUTER = Y + 2 * Y * Y

f32 = jnp.float32
bf16 = jnp.bfloat16
VMEM = pl.BlockSpec(memory_space=pltpu.VMEM)


def place():
    pair = lax.axis_index("pair")
    return pair // 2, pair % 2, lax.axis_index("rng") % 2 == 1


def starts():
    return [sum(SHARES[:y]) for y in range(Y)], [sum(SHARES[y + 1 :]) for y in range(Y)]


def start_of(y, odd):
    even_tile, odd_tile = starts()
    return jnp.where(odd, odd_tile[y], even_tile[y])


def base_of(y, odd):
    even_tile, odd_tile = ([start * LANES // RG_STEP - 1 for start in tile] for tile in starts())
    return jnp.where(odd, odd_tile[y], even_tile[y])


def pick(y, values):
    out = jnp.int32(values[0])
    for i in range(1, Y):
        out = jnp.where(y == i, values[i], out)
    return out


def lanes(rows):
    return lax.broadcasted_iota(jnp.int32, (rows, LANES), 1)


def azimuth_weights():
    line = lax.broadcasted_iota(jnp.int32, (LINES, LANES), 0)
    weights = []
    for look in range(LINES // AZ_STEP):
        offset = line - (AZ_STEP * look + (AZ_STEP - AZ_TAPS) // 2)
        centred = (offset.astype(f32) - (AZ_TAPS - 1) / 2.0) / (AZ_TAPS / 4.0)
        inside = (offset >= 0) & (offset < AZ_TAPS)
        weights.append(jnp.where(inside, jnp.exp(-0.5 * centred * centred), 0.0))
    return weights


def range_weights(y, odd):
    shape = (BLOCKS * LANES, LANES)
    row = lax.broadcasted_iota(jnp.int32, shape, 0)
    column = lax.broadcasted_iota(jnp.int32, shape, 1) % WINDOW
    look = column + pick(y, [base_of(i, odd) for i in range(Y)])
    start = pick(y, [start_of(i, odd) for i in range(Y)])
    count = pick(y, SHARES) * LANES
    halo = row - (BLOCKS - 1) * LANES
    beyond = halo + jnp.where(odd, sum(SHARES) * LANES, -RG_STEP)
    own = row < count
    sample = jnp.where(own, start * LANES + row, beyond)
    tap = sample - RG_STEP * (look - 1)
    centred = (tap.astype(f32) - (RG_TAPS - 1) / 2.0) / (RG_TAPS / 4.0)
    inside = (tap >= 0) & (tap < RG_TAPS) & (own | ((y == 0) & (halo >= 0) & (halo < RG_STEP)))
    return jnp.where(inside, 2.0 * jnp.exp(-0.5 * centred * centred), 0.0)


def cut_kernel(stack_ref, out_ref):
    _, _, odd = place()
    for y in range(Y):
        start = start_of(y, odd)
        for part in range(2):
            for t in range(BLOCKS):
                if t < SHARES[y]:
                    at = pl.multiple_of((start + t) * LANES, LANES)
                    out_ref[y, part, t] = stack_ref[0, part, :, pl.ds(at, LANES)]
                else:
                    out_ref[y, part, t] = jnp.zeros((LINES, LANES), bf16)


def edge_kernel(group_ref, edge_ref):
    _, _, odd = place()
    for part in range(2):
        packed = jnp.zeros((LINES, LANES), f32)
        for i in range(Y):
            first = group_ref[i, part, 0].astype(f32)
            last = group_ref[i, part, SHARES[0] - 1].astype(f32)
            edge = jnp.where(odd, pltpu.roll(last, RG_STEP, 1), first)
            edge = jnp.where(lanes(LINES) < RG_STEP, edge, 0.0)
            packed = packed + (pltpu.roll(edge, SLOT * i, 1) if i else edge)
        edge_ref[part] = packed.astype(bf16)


def join_kernel(group_ref, halo_ref, out_ref):
    share = SHARES[0]
    for i in range(Y):
        for part in range(2):
            for t in range(share):
                out_ref[(2 * i + part) * share + t] = group_ref[i, part, t]
    for part in range(2):
        out_ref[2 * Y * share + part] = halo_ref[part]


def unpack(packed, i):
    rolled = pltpu.roll(packed, LANES - SLOT * i, 1) if i else packed
    return jnp.where(lanes(LINES) < RG_STEP, rolled, 0.0)


def dates_at(ref, t, halos, joined_ref=None):
    def one(i, part):
        value = ref[i, part, t].astype(f32)
        if joined_ref is not None and t < SHARES[0]:
            value = value + joined_ref[(2 * i + part) * SHARES[0] + t].astype(f32)
        if t == BLOCKS - 1:
            value = value + unpack(halos[part], i)
        return value

    return [(one(i, 0), one(i, 1)) for i in range(Y)]


def power(date):
    x, y = date
    return ((0.5 * x) * x + (0.5 * y) * y,)


def cross(row, column):
    hx, hy = 0.5 * row[0], 0.5 * row[1]
    x, y = column
    return hx * x + hy * y, hy * x - hx * y


def put(x_ref, fields, t, values):
    at = t * LANES
    for field, value in enumerate(values):
        high = value.astype(bf16)
        low = (value - high.astype(f32)).astype(bf16)
        x_ref[field * LINES : (field + 1) * LINES, at : at + LANES] = high
        x_ref[(fields + field) * LINES : (fields + field + 1) * LINES, at : at + LANES] = low


def looks_of(x_ref, weights, d_ref, fields):
    d_ref[...] = jnp.dot(x_ref[...], weights, preferred_element_type=f32)
    azimuth = azimuth_weights()
    for field in range(fields):
        high = d_ref[field * LINES : (field + 1) * LINES, :]
        low = d_ref[(fields + field) * LINES : (fields + field + 1) * LINES, :]
        both = high + low
        summed = both + pltpu.roll(both, WINDOW, 1)
        for a, weight in enumerate(azimuth):
            yield field, a, jnp.sum(summed * weight, axis=0, keepdims=True)


def inner_kernel(group_ref, halo_ref, out_ref, weight_ref, x_ref, d_ref):
    y, _, odd = place()
    weights = range_weights(y, odd)
    high = weights.astype(bf16)
    low = (weights - high.astype(f32)).astype(bf16)
    column = lax.broadcasted_iota(jnp.int32, weights.shape, 1)
    weight_ref[...] = jnp.where(column < WINDOW, high.astype(f32), low.astype(f32)).astype(bf16)
    halos = [halo_ref[part].astype(f32) for part in range(2)]
    for t in range(BLOCKS):
        group = dates_at(group_ref, t, halos)
        fields = [power(d) for d in group] + [cross(group[i], group[j]) for i, j in INNER]
        put(x_ref, N_INNER, t, [value for field in fields for value in field])
    for field, a, row in looks_of(x_ref, weight_ref[...], d_ref, N_INNER):
        out_ref[2 * field + a : 2 * field + a + 1, :] = row


def outer_kernel(group_ref, halo_ref, other_ref, joined_ref, weight_ref, inner_ref, out_ref, x_ref, d_ref):
    _, own, _ = place()
    halos = [halo_ref[part].astype(f32) for part in range(2)]
    other_halos = [joined_ref[2 * Y * SHARES[0] + part].astype(f32) for part in range(2)]
    for t in range(BLOCKS):
        group, other = dates_at(group_ref, t, halos), dates_at(other_ref, t, other_halos, joined_ref)
        fields = [power(d) for d in other] + [cross(i, j) for i in group for j in other]
        put(x_ref, N_OUTER, t, [value for field in fields for value in field])

    first = lanes(1) < WINDOW
    mine = (first & (own == 0)) | (~first & (own == 1))

    def inner(field, a):
        return inner_ref[2 * field + a : 2 * field + a + 1, :]

    def inner_part(i, j, part, a):
        if i == j:
            return inner(i, a) if part == 0 else jnp.zeros((1, LANES), f32)
        field = Y + 2 * INNER.index((min(i, j), max(i, j))) + part
        return -inner(field, a) if part == 1 and i > j else inner(field, a)

    for field, a, row in looks_of(x_ref, weight_ref[...], d_ref, N_OUTER):
        if field < Y:
            at = 16 + 2 * field + a
            row = jnp.where(mine, inner(field, a), row)
            for i in range(Y):
                out_ref[i, at : at + 1, :] = row
        else:
            i, j = divmod((field - Y) // 2, Y)
            part = (field - Y) % 2
            at = 8 * part + 2 * j + a
            out_ref[i, at : at + 1, :] = jnp.where(mine, inner_part(i, j, part, a), row)


def normalise_kernel(parts_ref, out_ref):
    y, own, odd = place()
    rows = parts_ref.shape[1]
    lane = lanes(rows)
    first = lane < WINDOW
    end = jnp.where(odd, 0, LOOKS - 1)
    own_tile = jnp.where(odd, Y, 0)
    sides = []
    for side in range(2):

        def window(part, base):
            part = jnp.where(first == (side == 0), part, 0.0)
            return pltpu.roll(part, (base + 2 * LANES - side * WINDOW) % LANES, 1)

        summed = window(parts_ref[Y - own_tile + Y - 1], base_of(Y - 1, ~odd))
        summed = jnp.where(lane == end, summed, 0.0)
        for i in range(Y):
            base = base_of(i, odd)
            inside = (lane >= base) & (lane < base + WINDOW)
            summed = summed + jnp.where(inside, window(parts_ref[own_tile + i], base), 0.0)
        sides.append(summed)
    column_powers = [summed[16:24] for summed in sides]
    row_power = jnp.where(own == 0, *column_powers)
    row = lax.broadcasted_iota(jnp.int32, row_power.shape, 0)
    row_power = jnp.where(row // 2 == y, row_power, 0.0)
    row_power = row_power + pltpu.roll(row_power, 4, 0)
    row_power = row_power + pltpu.roll(row_power, 2, 0)
    for side in range(2):
        scale = lax.rsqrt((row_power + EPSILON) * (column_powers[side] + EPSILON))
        for k in range(2):
            values = sides[side][8 * k : 8 * k + 8] * scale
            for j in range(Y):
                out_ref[2 * j + side, k] = values[2 * j : 2 * j + 2]


def call(kernel, out_shape, operands, scratch=(), flops=0):
    return pl.pallas_call(
        kernel,
        out_shape=out_shape,
        in_specs=[VMEM] * len(operands),
        out_specs=jax.tree.map(lambda _: VMEM, out_shape),
        scratch_shapes=list(scratch),
        compiler_params=pltpu.CompilerParams(vmem_limit_bytes=VMEM_LIMIT),
        cost_estimate=pl.CostEstimate(flops=flops, bytes_accessed=1 << 20, transcendentals=0),
    )(*operands)


def looks(kernel, out_shape, operands, fields):
    rows, samples = 2 * fields * LINES, BLOCKS * LANES
    scratch = [pltpu.VMEM((rows, samples), bf16), pltpu.VMEM((rows, LANES), f32)]
    return call(kernel, out_shape, operands, scratch, flops=2 * rows * samples * LANES)


def local(stack):
    tiles = lax.axis_size("rng")
    axes = ("pair", "rng")

    def device(y, h, n):
        return (2 * y + h) * tiles + n

    def across(*ys):
        return [(device(y, h, n), device(y, 1 - h, n)) for y in ys for h in range(2) for n in range(tiles)]

    swap = []
    for h in range(2):
        for n in range(1, tiles - 1, 2):
            swap += [(device(0, h, n), device(0, h, n + 1)), (device(0, h, n + 1), device(0, h, n))]
    chips = [[device(y, h, n + c) for c in range(2) for y in range(Y)] for h in range(2) for n in range(0, tiles, 2)]

    chunks = call(cut_kernel, jax.ShapeDtypeStruct((Y, 2, BLOCKS, LINES, LANES), bf16), (stack,))
    group = lax.all_to_all(chunks, "pair", 0, 0, axis_index_groups=GROUPS)
    edge = call(edge_kernel, jax.ShapeDtypeStruct((2, LINES, LANES), bf16), (group,))
    group, edge = lax.optimization_barrier((group, edge))
    halo = lax.ppermute(edge, axes, swap)
    other = lax.ppermute(group, axes, across(1, 2, 3))
    joined = call(join_kernel, jax.ShapeDtypeStruct((2 * Y * SHARES[0] + 2, LINES, LANES), bf16), (group, halo))
    joined = lax.ppermute(joined, axes, across(0))

    shapes = (
        jax.ShapeDtypeStruct((2 * N_INNER, LANES), f32),
        jax.ShapeDtypeStruct((BLOCKS * LANES, LANES), bf16),
    )
    inner, weights = looks(inner_kernel, shapes, (group, halo), N_INNER)
    parts = looks(
        outer_kernel,
        jax.ShapeDtypeStruct((Y, 24, LANES), f32),
        (group, halo, other, joined, weights, inner),
        N_OUTER,
    )
    parts = lax.all_to_all(jnp.concatenate([parts, parts]), axes, 0, 0, axis_index_groups=chips)
    out = call(normalise_kernel, jax.ShapeDtypeStruct((2 * Y, 2, 2, LANES), f32), (parts,))
    return out[None]


def solution(mesh):
    in_specs = (P("pair", None, None, "rng"),)
    out_specs = P("pair", None, None, None, "rng")
    return jax.shard_map(local, mesh=mesh, in_specs=in_specs, out_specs=out_specs, check_vma=False)
```

```python
import jax
import jax.numpy as jnp
from jax import lax
from jax.experimental import pallas as pl
from jax.experimental.pallas import tpu as pltpu
from jax.sharding import PartitionSpec as P

AZ_TAPS = 31
RG_TAPS = 60
AZ_STEP = 8
RG_STEP = 20
LINES = 16
LANES = 128
SLOT = 32
WINDOW = 64
EPSILON = 1e-06
VMEM_LIMIT = 8 << 20

Y = 4
GROUPS = [[0, 2, 4, 6], [1, 3, 5, 7]]
INNER = [(i, j) for i in range(Y) for j in range(i + 1, Y)]
SHARES = (2, 6, 6, 6)
BLOCKS = max(SHARES)
LOOKS = sum(SHARES) * LANES // RG_STEP
N_INNER = Y + 2 * len(INNER)
N_OUTER = Y + 2 * Y * Y

f32 = jnp.float32
bf16 = jnp.bfloat16
VMEM = pl.BlockSpec(memory_space=pltpu.VMEM)


def place():
    pair = lax.axis_index("pair")
    return pair // 2, pair % 2, lax.axis_index("rng") % 2 == 1


def starts():
    return [sum(SHARES[:y]) for y in range(Y)], [sum(SHARES[y + 1 :]) for y in range(Y)]


def start_of(y, odd):
    even_tile, odd_tile = starts()
    return jnp.where(odd, odd_tile[y], even_tile[y])


def base_of(y, odd):
    even_tile, odd_tile = ([start * LANES // RG_STEP - 1 for start in tile] for tile in starts())
    return jnp.where(odd, odd_tile[y], even_tile[y])


def pick(y, values):
    out = jnp.int32(values[0])
    for i in range(1, Y):
        out = jnp.where(y == i, values[i], out)
    return out


def lanes(rows):
    return lax.broadcasted_iota(jnp.int32, (rows, LANES), 1)


def azimuth_weights():
    line = lax.broadcasted_iota(jnp.int32, (LINES, LANES), 0)
    weights = []
    for look in range(LINES // AZ_STEP):
        offset = line - (AZ_STEP * look + (AZ_STEP - AZ_TAPS) // 2)
        centred = (offset.astype(f32) - (AZ_TAPS - 1) / 2.0) / (AZ_TAPS / 4.0)
        inside = (offset >= 0) & (offset < AZ_TAPS)
        weights.append(jnp.where(inside, jnp.exp(-0.5 * centred * centred), 0.0))
    return weights


def range_weights(y, odd):
    shape = (BLOCKS * LANES, LANES)
    row = lax.broadcasted_iota(jnp.int32, shape, 0)
    column = lax.broadcasted_iota(jnp.int32, shape, 1) % WINDOW
    look = column + pick(y, [base_of(i, odd) for i in range(Y)])
    start = pick(y, [start_of(i, odd) for i in range(Y)])
    count = pick(y, SHARES) * LANES
    halo = row - (BLOCKS - 1) * LANES
    beyond = halo + jnp.where(odd, sum(SHARES) * LANES, -RG_STEP)
    own = row < count
    sample = jnp.where(own, start * LANES + row, beyond)
    tap = sample - RG_STEP * (look - 1)
    centred = (tap.astype(f32) - (RG_TAPS - 1) / 2.0) / (RG_TAPS / 4.0)
    inside = (tap >= 0) & (tap < RG_TAPS) & (own | ((y == 0) & (halo >= 0) & (halo < RG_STEP)))
    return jnp.where(inside, 2.0 * jnp.exp(-0.5 * centred * centred), 0.0)


def cut_kernel(stack_ref, out_ref):
    _, _, odd = place()
    for y in range(Y):
        start = start_of(y, odd)
        for part in range(2):
            for t in range(BLOCKS):
                if t < SHARES[y]:
                    at = pl.multiple_of((start + t) * LANES, LANES)
                    out_ref[y, part, t] = stack_ref[0, part, :, pl.ds(at, LANES)]
                else:
                    out_ref[y, part, t] = jnp.zeros((LINES, LANES), bf16)


def edge_kernel(group_ref, edge_ref):
    _, _, odd = place()
    for part in range(2):
        packed = jnp.zeros((LINES, LANES), f32)
        for i in range(Y):
            first = group_ref[i, part, 0].astype(f32)
            last = group_ref[i, part, SHARES[0] - 1].astype(f32)
            edge = jnp.where(odd, pltpu.roll(last, RG_STEP, 1), first)
            edge = jnp.where(lanes(LINES) < RG_STEP, edge, 0.0)
            packed = packed + (pltpu.roll(edge, SLOT * i, 1) if i else edge)
        edge_ref[part] = packed.astype(bf16)


def join_kernel(group_ref, halo_ref, out_ref):
    share = SHARES[0]
    for i in range(Y):
        for part in range(2):
            for t in range(share):
                out_ref[(2 * i + part) * share + t] = group_ref[i, part, t]
    for part in range(2):
        out_ref[2 * Y * share + part] = halo_ref[part]


def unpack(packed, i):
    rolled = pltpu.roll(packed, LANES - SLOT * i, 1) if i else packed
    return jnp.where(lanes(LINES) < RG_STEP, rolled, 0.0)


def dates_at(ref, t, halos, joined_ref=None):
    def one(i, part):
        value = ref[i, part, t].astype(f32)
        if joined_ref is not None and t < SHARES[0]:
            value = value + joined_ref[(2 * i + part) * SHARES[0] + t].astype(f32)
        if t == BLOCKS - 1:
            value = value + unpack(halos[part], i)
        return value

    return [(one(i, 0), one(i, 1)) for i in range(Y)]


def power(date):
    x, y = date
    return ((0.5 * x) * x + (0.5 * y) * y,)


def cross(row, column):
    hx, hy = 0.5 * row[0], 0.5 * row[1]
    x, y = column
    return hx * x + hy * y, hy * x - hx * y


def put(x_ref, fields, t, values):
    at = t * LANES
    for field, value in enumerate(values):
        high = value.astype(bf16)
        low = (value - high.astype(f32)).astype(bf16)
        x_ref[field * LINES : (field + 1) * LINES, at : at + LANES] = high
        x_ref[(fields + field) * LINES : (fields + field + 1) * LINES, at : at + LANES] = low


def looks_of(x_ref, weights, d_ref, fields):
    d_ref[...] = jnp.dot(x_ref[...], weights, preferred_element_type=f32)
    azimuth = azimuth_weights()
    for field in range(fields):
        high = d_ref[field * LINES : (field + 1) * LINES, :]
        low = d_ref[(fields + field) * LINES : (fields + field + 1) * LINES, :]
        both = high + low
        summed = both + pltpu.roll(both, WINDOW, 1)
        for a, weight in enumerate(azimuth):
            yield field, a, jnp.sum(summed * weight, axis=0, keepdims=True)


def inner_kernel(group_ref, halo_ref, out_ref, weight_ref, x_ref, d_ref):
    y, _, odd = place()
    weights = range_weights(y, odd)
    high = weights.astype(bf16)
    low = (weights - high.astype(f32)).astype(bf16)
    column = lax.broadcasted_iota(jnp.int32, weights.shape, 1)
    weight_ref[...] = jnp.where(column < WINDOW, high.astype(f32), low.astype(f32)).astype(bf16)
    halos = [halo_ref[part].astype(f32) for part in range(2)]
    for t in range(BLOCKS):
        group = dates_at(group_ref, t, halos)
        fields = [power(d) for d in group] + [cross(group[i], group[j]) for i, j in INNER]
        put(x_ref, N_INNER, t, [value for field in fields for value in field])
    for field, a, row in looks_of(x_ref, weight_ref[...], d_ref, N_INNER):
        out_ref[2 * field + a : 2 * field + a + 1, :] = row


def outer_kernel(group_ref, halo_ref, other_ref, joined_ref, weight_ref, inner_ref, out_ref, x_ref, d_ref):
    _, own, _ = place()
    halos = [halo_ref[part].astype(f32) for part in range(2)]
    other_halos = [joined_ref[2 * Y * SHARES[0] + part].astype(f32) for part in range(2)]
    for t in range(BLOCKS):
        group, other = dates_at(group_ref, t, halos), dates_at(other_ref, t, other_halos, joined_ref)
        fields = [power(d) for d in other] + [cross(i, j) for i in group for j in other]
        put(x_ref, N_OUTER, t, [value for field in fields for value in field])

    first = lanes(1) < WINDOW
    mine = (first & (own == 0)) | (~first & (own == 1))

    def inner(field, a):
        return inner_ref[2 * field + a : 2 * field + a + 1, :]

    def inner_part(i, j, part, a):
        if i == j:
            return inner(i, a) if part == 0 else jnp.zeros((1, LANES), f32)
        field = Y + 2 * INNER.index((min(i, j), max(i, j))) + part
        return -inner(field, a) if part == 1 and i > j else inner(field, a)

    for field, a, row in looks_of(x_ref, weight_ref[...], d_ref, N_OUTER):
        if field < Y:
            at = 16 + 2 * field + a
            row = jnp.where(mine, inner(field, a), row)
            for i in range(Y):
                out_ref[i, at : at + 1, :] = row
        else:
            i, j = divmod((field - Y) // 2, Y)
            part = (field - Y) % 2
            at = 8 * part + 2 * j + a
            out_ref[i, at : at + 1, :] = jnp.where(mine, inner_part(i, j, part, a), row)


def normalise_kernel(parts_ref, out_ref):
    y, own, odd = place()
    rows = parts_ref.shape[1]
    lane = lanes(rows)
    first = lane < WINDOW
    end = jnp.where(odd, 0, LOOKS - 1)
    own_tile = jnp.where(odd, Y, 0)
    sides = []
    for side in range(2):

        def window(part, base):
            part = jnp.where(first == (side == 0), part, 0.0)
            return pltpu.roll(part, (base + 2 * LANES - side * WINDOW) % LANES, 1)

        summed = window(parts_ref[Y - own_tile + Y - 1], base_of(Y - 1, ~odd))
        summed = jnp.where(lane == end, summed, 0.0)
        for i in range(Y):
            base = base_of(i, odd)
            inside = (lane >= base) & (lane < base + WINDOW)
            summed = summed + jnp.where(inside, window(parts_ref[own_tile + i], base), 0.0)
        sides.append(summed)
    column_powers = [summed[16:24] for summed in sides]
    row_power = jnp.where(own == 0, *column_powers)
    row = lax.broadcasted_iota(jnp.int32, row_power.shape, 0)
    row_power = jnp.where(row // 2 == y, row_power, 0.0)
    row_power = row_power + pltpu.roll(row_power, 4, 0)
    row_power = row_power + pltpu.roll(row_power, 2, 0)
    for side in range(2):
        scale = lax.rsqrt((row_power + EPSILON) * (column_powers[side] + EPSILON))
        for k in range(2):
            values = sides[side][8 * k : 8 * k + 8] * scale
            for j in range(Y):
                out_ref[2 * j + side, k] = values[2 * j : 2 * j + 2]


def call(kernel, out_shape, operands, scratch=(), flops=0):
    return pl.pallas_call(
        kernel,
        out_shape=out_shape,
        in_specs=[VMEM] * len(operands),
        out_specs=jax.tree.map(lambda _: VMEM, out_shape),
        scratch_shapes=list(scratch),
        compiler_params=pltpu.CompilerParams(vmem_limit_bytes=VMEM_LIMIT),
        cost_estimate=pl.CostEstimate(flops=flops, bytes_accessed=1 << 20, transcendentals=0),
    )(*operands)


def looks(kernel, out_shape, operands, fields):
    rows, samples = 2 * fields * LINES, BLOCKS * LANES
    scratch = [pltpu.VMEM((rows, samples), bf16), pltpu.VMEM((rows, LANES), f32)]
    return call(kernel, out_shape, operands, scratch, flops=2 * rows * samples * LANES)


def local(stack):
    tiles = lax.axis_size("rng")
    axes = ("pair", "rng")

    def device(y, h, n):
        return (2 * y + h) * tiles + n

    def across(*ys):
        return [(device(y, h, n), device(y, 1 - h, n)) for y in ys for h in range(2) for n in range(tiles)]

    swap = []
    for h in range(2):
        for n in range(1, tiles - 1, 2):
            swap += [(device(0, h, n), device(0, h, n + 1)), (device(0, h, n + 1), device(0, h, n))]
    chips = [[device(y, h, n + c) for c in range(2) for y in range(Y)] for h in range(2) for n in range(0, tiles, 2)]

    chunks = call(cut_kernel, jax.ShapeDtypeStruct((Y, 2, BLOCKS, LINES, LANES), bf16), (stack,))
    group = lax.all_to_all(chunks, "pair", 0, 0, axis_index_groups=GROUPS)
    edge = call(edge_kernel, jax.ShapeDtypeStruct((2, LINES, LANES), bf16), (group,))
    halo = lax.ppermute(edge, axes, swap)
    other = lax.ppermute(group, axes, across(1, 2, 3))
    joined = call(join_kernel, jax.ShapeDtypeStruct((2 * Y * SHARES[0] + 2, LINES, LANES), bf16), (group, halo))
    joined = lax.ppermute(joined, axes, across(0))

    shapes = (
        jax.ShapeDtypeStruct((2 * N_INNER, LANES), f32),
        jax.ShapeDtypeStruct((BLOCKS * LANES, LANES), bf16),
    )
    inner, weights = looks(inner_kernel, shapes, (group, halo), N_INNER)
    parts = looks(
        outer_kernel,
        jax.ShapeDtypeStruct((Y, 24, LANES), f32),
        (group, halo, other, joined, weights, inner),
        N_OUTER,
    )
    parts = lax.all_to_all(jnp.concatenate([parts, parts]), axes, 0, 0, axis_index_groups=chips)
    out = call(normalise_kernel, jax.ShapeDtypeStruct((2 * Y, 2, 2, LANES), f32), (parts,))
    return out[None]


def solution(mesh):
    in_specs = (P("pair", None, None, "rng"),)
    out_specs = P("pair", None, None, None, "rng")
    return jax.shard_map(local, mesh=mesh, in_specs=in_specs, out_specs=out_specs, check_vma=False)
```

```python
import jax
import jax.numpy as jnp
from jax import lax
from jax.experimental import pallas as pl
from jax.experimental.pallas import tpu as pltpu
from jax.sharding import PartitionSpec as P

AZ_TAPS = 31
RG_TAPS = 60
AZ_STEP = 8
RG_STEP = 20
LINES = 16
LANES = 128
SLOT = 32
WINDOW = 64
EPSILON = 1e-06
VMEM_LIMIT = 8 << 20

Y = 4
GROUPS = [[0, 2, 4, 6], [1, 3, 5, 7]]
INNER = [(i, j) for i in range(Y) for j in range(i + 1, Y)]
SHARES = (2, 6, 6, 6)
BLOCKS = max(SHARES)
LOOKS = sum(SHARES) * LANES // RG_STEP
N_INNER = Y + 2 * len(INNER)
N_OUTER = Y + 2 * Y * Y

f32 = jnp.float32
bf16 = jnp.bfloat16
VMEM = pl.BlockSpec(memory_space=pltpu.VMEM)


def place():
    pair = lax.axis_index("pair")
    return pair // 2, pair % 2, lax.axis_index("rng") % 2 == 1


def starts():
    return [sum(SHARES[:y]) for y in range(Y)], [sum(SHARES[y + 1 :]) for y in range(Y)]


def start_of(y, odd):
    even_tile, odd_tile = starts()
    return jnp.where(odd, odd_tile[y], even_tile[y])


def base_of(y, odd):
    even_tile, odd_tile = ([start * LANES // RG_STEP - 1 for start in tile] for tile in starts())
    return jnp.where(odd, odd_tile[y], even_tile[y])


def pick(y, values):
    out = jnp.int32(values[0])
    for i in range(1, Y):
        out = jnp.where(y == i, values[i], out)
    return out


def lanes(rows):
    return lax.broadcasted_iota(jnp.int32, (rows, LANES), 1)


def azimuth_weights():
    line = lax.broadcasted_iota(jnp.int32, (LINES, LANES), 0)
    weights = []
    for look in range(LINES // AZ_STEP):
        offset = line - (AZ_STEP * look + (AZ_STEP - AZ_TAPS) // 2)
        centred = (offset.astype(f32) - (AZ_TAPS - 1) / 2.0) / (AZ_TAPS / 4.0)
        inside = (offset >= 0) & (offset < AZ_TAPS)
        weights.append(jnp.where(inside, jnp.exp(-0.5 * centred * centred), 0.0))
    return weights


def range_weights(y, odd):
    shape = (BLOCKS * LANES, LANES)
    row = lax.broadcasted_iota(jnp.int32, shape, 0)
    column = lax.broadcasted_iota(jnp.int32, shape, 1) % WINDOW
    look = column + pick(y, [base_of(i, odd) for i in range(Y)])
    start = pick(y, [start_of(i, odd) for i in range(Y)])
    count = pick(y, SHARES) * LANES
    halo = row - (BLOCKS - 1) * LANES
    beyond = halo + jnp.where(odd, sum(SHARES) * LANES, -RG_STEP)
    own = row < count
    sample = jnp.where(own, start * LANES + row, beyond)
    tap = sample - RG_STEP * (look - 1)
    centred = (tap.astype(f32) - (RG_TAPS - 1) / 2.0) / (RG_TAPS / 4.0)
    inside = (tap >= 0) & (tap < RG_TAPS) & (own | ((y == 0) & (halo >= 0) & (halo < RG_STEP)))
    return jnp.where(inside, 2.0 * jnp.exp(-0.5 * centred * centred), 0.0)


def cut_kernel(stack_ref, out_ref):
    _, _, odd = place()
    for y in range(Y):
        start = start_of(y, odd)
        for part in range(2):
            for t in range(BLOCKS):
                if t < SHARES[y]:
                    at = pl.multiple_of((start + t) * LANES, LANES)
                    out_ref[y, part, t] = stack_ref[0, part, :, pl.ds(at, LANES)]
                else:
                    out_ref[y, part, t] = jnp.zeros((LINES, LANES), bf16)


def edge_kernel(group_ref, edge_ref):
    _, _, odd = place()
    for part in range(2):
        packed = jnp.zeros((LINES, LANES), f32)
        for i in range(Y):
            first = group_ref[i, part, 0].astype(f32)
            last = group_ref[i, part, SHARES[0] - 1].astype(f32)
            edge = jnp.where(odd, pltpu.roll(last, RG_STEP, 1), first)
            edge = jnp.where(lanes(LINES) < RG_STEP, edge, 0.0)
            packed = packed + (pltpu.roll(edge, SLOT * i, 1) if i else edge)
        edge_ref[part] = packed.astype(bf16)


def join_kernel(group_ref, halo_ref, out_ref):
    share = SHARES[0]
    for i in range(Y):
        for part in range(2):
            for t in range(share):
                out_ref[(2 * i + part) * share + t] = group_ref[i, part, t]
    for part in range(2):
        out_ref[2 * Y * share + part] = halo_ref[part]


def unpack(packed, i):
    rolled = pltpu.roll(packed, LANES - SLOT * i, 1) if i else packed
    return jnp.where(lanes(LINES) < RG_STEP, rolled, 0.0)


def dates_at(refs, t, halos, joined_ref=None):
    def one(i, part):
        value = sum(ref[i, part, t].astype(f32) for ref in refs)
        if joined_ref is not None and t < SHARES[0]:
            value = value + joined_ref[(2 * i + part) * SHARES[0] + t].astype(f32)
        if t == BLOCKS - 1:
            value = value + unpack(halos[part], i)
        return value

    return [(one(i, 0), one(i, 1)) for i in range(Y)]


def power(date):
    x, y = date
    return ((0.5 * x) * x + (0.5 * y) * y,)


def cross(row, column):
    hx, hy = 0.5 * row[0], 0.5 * row[1]
    x, y = column
    return hx * x + hy * y, hy * x - hx * y


def put(x_ref, fields, t, values):
    at = t * LANES
    for field, value in enumerate(values):
        high = value.astype(bf16)
        low = (value - high.astype(f32)).astype(bf16)
        x_ref[field * LINES : (field + 1) * LINES, at : at + LANES] = high
        x_ref[(fields + field) * LINES : (fields + field + 1) * LINES, at : at + LANES] = low


def looks_of(x_ref, weights, d_ref, fields):
    d_ref[...] = jnp.dot(x_ref[...], weights, preferred_element_type=f32)
    azimuth = azimuth_weights()
    for field in range(fields):
        high = d_ref[field * LINES : (field + 1) * LINES, :]
        low = d_ref[(fields + field) * LINES : (fields + field + 1) * LINES, :]
        both = high + low
        summed = both + pltpu.roll(both, WINDOW, 1)
        for a, weight in enumerate(azimuth):
            yield field, a, jnp.sum(summed * weight, axis=0, keepdims=True)


def inner_kernel(group_ref, halo_ref, out_ref, weight_ref, x_ref, d_ref):
    y, _, odd = place()
    weights = range_weights(y, odd)
    high = weights.astype(bf16)
    low = (weights - high.astype(f32)).astype(bf16)
    column = lax.broadcasted_iota(jnp.int32, weights.shape, 1)
    weight_ref[...] = jnp.where(column < WINDOW, high.astype(f32), low.astype(f32)).astype(bf16)
    halos = [halo_ref[part].astype(f32) for part in range(2)]
    for t in range(BLOCKS):
        group = dates_at([group_ref], t, halos)
        fields = [power(d) for d in group] + [cross(group[i], group[j]) for i, j in INNER]
        put(x_ref, N_INNER, t, [value for field in fields for value in field])
    for field, a, row in looks_of(x_ref, weight_ref[...], d_ref, N_INNER):
        out_ref[2 * field + a : 2 * field + a + 1, :] = row


def outer_kernel(group_ref, halo_ref, even_ref, odd_ref, joined_ref, weight_ref, inner_ref, out_ref, x_ref, d_ref):
    _, own, _ = place()
    halos = [halo_ref[part].astype(f32) for part in range(2)]
    other_halos = [joined_ref[2 * Y * SHARES[0] + part].astype(f32) for part in range(2)]
    for t in range(BLOCKS):
        group, other = dates_at([group_ref], t, halos), dates_at([even_ref, odd_ref], t, other_halos, joined_ref)
        fields = [power(d) for d in other] + [cross(i, j) for i in group for j in other]
        put(x_ref, N_OUTER, t, [value for field in fields for value in field])

    first = lanes(1) < WINDOW
    mine = (first & (own == 0)) | (~first & (own == 1))

    def inner(field, a):
        return inner_ref[2 * field + a : 2 * field + a + 1, :]

    def inner_part(i, j, part, a):
        if i == j:
            return inner(i, a) if part == 0 else jnp.zeros((1, LANES), f32)
        field = Y + 2 * INNER.index((min(i, j), max(i, j))) + part
        return -inner(field, a) if part == 1 and i > j else inner(field, a)

    for field, a, row in looks_of(x_ref, weight_ref[...], d_ref, N_OUTER):
        if field < Y:
            at = 16 + 2 * field + a
            row = jnp.where(mine, inner(field, a), row)
            for i in range(Y):
                out_ref[i, at : at + 1, :] = row
        else:
            i, j = divmod((field - Y) // 2, Y)
            part = (field - Y) % 2
            at = 8 * part + 2 * j + a
            out_ref[i, at : at + 1, :] = jnp.where(mine, inner_part(i, j, part, a), row)


def normalise_kernel(parts_ref, out_ref):
    y, own, odd = place()
    rows = parts_ref.shape[1]
    lane = lanes(rows)
    first = lane < WINDOW
    end = jnp.where(odd, 0, LOOKS - 1)
    own_tile = jnp.where(odd, Y, 0)
    sides = []
    for side in range(2):

        def window(part, base):
            part = jnp.where(first == (side == 0), part, 0.0)
            return pltpu.roll(part, (base + 2 * LANES - side * WINDOW) % LANES, 1)

        summed = window(parts_ref[Y - own_tile + Y - 1], base_of(Y - 1, ~odd))
        summed = jnp.where(lane == end, summed, 0.0)
        for i in range(Y):
            base = base_of(i, odd)
            inside = (lane >= base) & (lane < base + WINDOW)
            summed = summed + jnp.where(inside, window(parts_ref[own_tile + i], base), 0.0)
        sides.append(summed)
    column_powers = [summed[16:24] for summed in sides]
    row_power = jnp.where(own == 0, *column_powers)
    row = lax.broadcasted_iota(jnp.int32, row_power.shape, 0)
    row_power = jnp.where(row // 2 == y, row_power, 0.0)
    row_power = row_power + pltpu.roll(row_power, 4, 0)
    row_power = row_power + pltpu.roll(row_power, 2, 0)
    for side in range(2):
        scale = lax.rsqrt((row_power + EPSILON) * (column_powers[side] + EPSILON))
        for k in range(2):
            values = sides[side][8 * k : 8 * k + 8] * scale
            for j in range(Y):
                out_ref[2 * j + side, k] = values[2 * j : 2 * j + 2]


def call(kernel, out_shape, operands, scratch=(), flops=0):
    return pl.pallas_call(
        kernel,
        out_shape=out_shape,
        in_specs=[VMEM] * len(operands),
        out_specs=jax.tree.map(lambda _: VMEM, out_shape),
        scratch_shapes=list(scratch),
        compiler_params=pltpu.CompilerParams(vmem_limit_bytes=VMEM_LIMIT),
        cost_estimate=pl.CostEstimate(flops=flops, bytes_accessed=1 << 20, transcendentals=0),
    )(*operands)


def looks(kernel, out_shape, operands, fields):
    rows, samples = 2 * fields * LINES, BLOCKS * LANES
    scratch = [pltpu.VMEM((rows, samples), bf16), pltpu.VMEM((rows, LANES), f32)]
    return call(kernel, out_shape, operands, scratch, flops=2 * rows * samples * LANES)


def local(stack):
    tiles = lax.axis_size("rng")
    axes = ("pair", "rng")

    def device(y, h, n):
        return (2 * y + h) * tiles + n

    def across(ys, cores=(0, 1)):
        pairs = [(y, h, n) for y in ys for h in range(2) for n in range(tiles) if n % 2 in cores]
        return [(device(y, h, n), device(y, 1 - h, n)) for y, h, n in pairs]

    swap = []
    for h in range(2):
        for n in range(1, tiles - 1, 2):
            swap += [(device(0, h, n), device(0, h, n + 1)), (device(0, h, n + 1), device(0, h, n))]
    chips = [[device(y, h, n + c) for c in range(2) for y in range(Y)] for h in range(2) for n in range(0, tiles, 2)]

    chunks = call(cut_kernel, jax.ShapeDtypeStruct((Y, 2, BLOCKS, LINES, LANES), bf16), (stack,))
    group = lax.all_to_all(chunks, "pair", 0, 0, axis_index_groups=GROUPS)
    edge = call(edge_kernel, jax.ShapeDtypeStruct((2, LINES, LANES), bf16), (group,))
    halo = lax.ppermute(edge, axes, swap)
    others = [lax.ppermute(group, axes, across((1, 2, 3), (core,))) for core in range(2)]
    joined = call(join_kernel, jax.ShapeDtypeStruct((2 * Y * SHARES[0] + 2, LINES, LANES), bf16), (group, halo))
    joined = lax.ppermute(joined, axes, across((0,)))

    shapes = (
        jax.ShapeDtypeStruct((2 * N_INNER, LANES), f32),
        jax.ShapeDtypeStruct((BLOCKS * LANES, LANES), bf16),
    )
    inner, weights = looks(inner_kernel, shapes, (group, halo), N_INNER)
    parts = looks(
        outer_kernel,
        jax.ShapeDtypeStruct((Y, 24, LANES), f32),
        (group, halo, *others, joined, weights, inner),
        N_OUTER,
    )
    parts = lax.all_to_all(jnp.concatenate([parts, parts]), axes, 0, 0, axis_index_groups=chips)
    out = call(normalise_kernel, jax.ShapeDtypeStruct((2 * Y, 2, 2, LANES), f32), (parts,))
    return out[None]


def solution(mesh):
    in_specs = (P("pair", None, None, "rng"),)
    out_specs = P("pair", None, None, None, "rng")
    return jax.shard_map(local, mesh=mesh, in_specs=in_specs, out_specs=out_specs, check_vma=False)
```

```python
import jax
import jax.numpy as jnp
from jax import lax
from jax.experimental import pallas as pl
from jax.experimental.pallas import tpu as pltpu
from jax.sharding import PartitionSpec as P

AZ_TAPS = 31
RG_TAPS = 60
AZ_STEP = 8
RG_STEP = 20
LINES = 16
LANES = 128
SLOT = 32
WINDOW = 64
EPSILON = 1e-06
VMEM_LIMIT = 8 << 20

Y = 4
GROUPS = [[0, 2, 4, 6], [1, 3, 5, 7]]
INNER = [(i, j) for i in range(Y) for j in range(i + 1, Y)]
SHARES = (2, 6, 6, 6)
BLOCKS = max(SHARES)
LOOKS = sum(SHARES) * LANES // RG_STEP
N_INNER = Y + 2 * len(INNER)
N_OUTER = Y + 2 * Y * Y

f32 = jnp.float32
bf16 = jnp.bfloat16
VMEM = pl.BlockSpec(memory_space=pltpu.VMEM)


def place():
    pair = lax.axis_index("pair")
    return pair // 2, pair % 2, lax.axis_index("rng") % 2 == 1


def starts():
    return [sum(SHARES[:y]) for y in range(Y)], [sum(SHARES[y + 1 :]) for y in range(Y)]


def start_of(y, odd):
    even_tile, odd_tile = starts()
    return jnp.where(odd, odd_tile[y], even_tile[y])


def base_of(y, odd):
    even_tile, odd_tile = ([start * LANES // RG_STEP - 1 for start in tile] for tile in starts())
    return jnp.where(odd, odd_tile[y], even_tile[y])


def pick(y, values):
    out = jnp.int32(values[0])
    for i in range(1, Y):
        out = jnp.where(y == i, values[i], out)
    return out


def lanes(rows):
    return lax.broadcasted_iota(jnp.int32, (rows, LANES), 1)


def azimuth_weights():
    line = lax.broadcasted_iota(jnp.int32, (LINES, LANES), 0)
    weights = []
    for look in range(LINES // AZ_STEP):
        offset = line - (AZ_STEP * look + (AZ_STEP - AZ_TAPS) // 2)
        centred = (offset.astype(f32) - (AZ_TAPS - 1) / 2.0) / (AZ_TAPS / 4.0)
        inside = (offset >= 0) & (offset < AZ_TAPS)
        weights.append(jnp.where(inside, jnp.exp(-0.5 * centred * centred), 0.0))
    return weights


def range_weights(y, odd):
    shape = (BLOCKS * LANES, LANES)
    row = lax.broadcasted_iota(jnp.int32, shape, 0)
    column = lax.broadcasted_iota(jnp.int32, shape, 1) % WINDOW
    look = column + pick(y, [base_of(i, odd) for i in range(Y)])
    start = pick(y, [start_of(i, odd) for i in range(Y)])
    count = pick(y, SHARES) * LANES
    halo = row - (BLOCKS - 1) * LANES
    beyond = halo + jnp.where(odd, sum(SHARES) * LANES, -RG_STEP)
    own = row < count
    sample = jnp.where(own, start * LANES + row, beyond)
    tap = sample - RG_STEP * (look - 1)
    centred = (tap.astype(f32) - (RG_TAPS - 1) / 2.0) / (RG_TAPS / 4.0)
    inside = (tap >= 0) & (tap < RG_TAPS) & (own | ((y == 0) & (halo >= 0) & (halo < RG_STEP)))
    return jnp.where(inside, 2.0 * jnp.exp(-0.5 * centred * centred), 0.0)


def cut_kernel(stack_ref, out_ref):
    _, _, odd = place()
    for y in range(Y):
        start = start_of(y, odd)
        for part in range(2):
            for t in range(BLOCKS):
                if t < SHARES[y]:
                    at = pl.multiple_of((start + t) * LANES, LANES)
                    out_ref[y, part, t] = stack_ref[0, part, :, pl.ds(at, LANES)]
                else:
                    out_ref[y, part, t] = jnp.zeros((LINES, LANES), bf16)


def edge_kernel(group_ref, edge_ref):
    _, _, odd = place()
    for part in range(2):
        packed = jnp.zeros((LINES, LANES), f32)
        for i in range(Y):
            first = group_ref[i, part, 0].astype(f32)
            last = group_ref[i, part, SHARES[0] - 1].astype(f32)
            edge = jnp.where(odd, pltpu.roll(last, RG_STEP, 1), first)
            edge = jnp.where(lanes(LINES) < RG_STEP, edge, 0.0)
            packed = packed + (pltpu.roll(edge, SLOT * i, 1) if i else edge)
        edge_ref[part] = packed.astype(bf16)


def join_kernel(group_ref, halo_ref, out_ref):
    share = SHARES[0]
    for i in range(Y):
        for part in range(2):
            for t in range(share):
                out_ref[(2 * i + part) * share + t] = group_ref[i, part, t]
    for part in range(2):
        out_ref[2 * Y * share + part] = halo_ref[part]


def unpack(packed, i):
    rolled = pltpu.roll(packed, LANES - SLOT * i, 1) if i else packed
    return jnp.where(lanes(LINES) < RG_STEP, rolled, 0.0)


def dates_at(refs, t, halos, joined_refs=()):
    def one(i, part):
        value = sum(ref[i, part, t].astype(f32) for ref in refs)
        if t < SHARES[0]:
            value = value + sum(ref[(2 * i + part) * SHARES[0] + t].astype(f32) for ref in joined_refs)
        if t == BLOCKS - 1:
            value = value + unpack(halos[part], i)
        return value

    return [(one(i, 0), one(i, 1)) for i in range(Y)]


def power(date):
    x, y = date
    return ((0.5 * x) * x + (0.5 * y) * y,)


def cross(row, column):
    hx, hy = 0.5 * row[0], 0.5 * row[1]
    x, y = column
    return hx * x + hy * y, hy * x - hx * y


def put(x_ref, fields, t, values):
    at = t * LANES
    for field, value in enumerate(values):
        high = value.astype(bf16)
        low = (value - high.astype(f32)).astype(bf16)
        x_ref[field * LINES : (field + 1) * LINES, at : at + LANES] = high
        x_ref[(fields + field) * LINES : (fields + field + 1) * LINES, at : at + LANES] = low


def looks_of(x_ref, weights, d_ref, fields):
    d_ref[...] = jnp.dot(x_ref[...], weights, preferred_element_type=f32)
    azimuth = azimuth_weights()
    for field in range(fields):
        high = d_ref[field * LINES : (field + 1) * LINES, :]
        low = d_ref[(fields + field) * LINES : (fields + field + 1) * LINES, :]
        both = high + low
        summed = both + pltpu.roll(both, WINDOW, 1)
        for a, weight in enumerate(azimuth):
            yield field, a, jnp.sum(summed * weight, axis=0, keepdims=True)


def inner_kernel(group_ref, halo_ref, out_ref, weight_ref, x_ref, d_ref):
    y, _, odd = place()
    weights = range_weights(y, odd)
    high = weights.astype(bf16)
    low = (weights - high.astype(f32)).astype(bf16)
    column = lax.broadcasted_iota(jnp.int32, weights.shape, 1)
    weight_ref[...] = jnp.where(column < WINDOW, high.astype(f32), low.astype(f32)).astype(bf16)
    halos = [halo_ref[part].astype(f32) for part in range(2)]
    for t in range(BLOCKS):
        group = dates_at([group_ref], t, halos)
        fields = [power(d) for d in group] + [cross(group[i], group[j]) for i, j in INNER]
        put(x_ref, N_INNER, t, [value for field in fields for value in field])
    for field, a, row in looks_of(x_ref, weight_ref[...], d_ref, N_INNER):
        out_ref[2 * field + a : 2 * field + a + 1, :] = row


def outer_kernel(group_ref, halo_ref, even_ref, odd_ref, *refs):
    *joined_refs, weight_ref, inner_ref, out_ref, x_ref, d_ref = refs
    _, own, _ = place()
    halos = [halo_ref[part].astype(f32) for part in range(2)]
    other_halos = [sum(ref[2 * Y * SHARES[0] + part].astype(f32) for ref in joined_refs) for part in range(2)]
    for t in range(BLOCKS):
        group, other = dates_at([group_ref], t, halos), dates_at([even_ref, odd_ref], t, other_halos, joined_refs)
        fields = [power(d) for d in other] + [cross(i, j) for i in group for j in other]
        put(x_ref, N_OUTER, t, [value for field in fields for value in field])

    first = lanes(1) < WINDOW
    mine = (first & (own == 0)) | (~first & (own == 1))

    def inner(field, a):
        return inner_ref[2 * field + a : 2 * field + a + 1, :]

    def inner_part(i, j, part, a):
        if i == j:
            return inner(i, a) if part == 0 else jnp.zeros((1, LANES), f32)
        field = Y + 2 * INNER.index((min(i, j), max(i, j))) + part
        return -inner(field, a) if part == 1 and i > j else inner(field, a)

    for field, a, row in looks_of(x_ref, weight_ref[...], d_ref, N_OUTER):
        if field < Y:
            at = 16 + 2 * field + a
            row = jnp.where(mine, inner(field, a), row)
            for i in range(Y):
                out_ref[i, at : at + 1, :] = row
        else:
            i, j = divmod((field - Y) // 2, Y)
            part = (field - Y) % 2
            at = 8 * part + 2 * j + a
            out_ref[i, at : at + 1, :] = jnp.where(mine, inner_part(i, j, part, a), row)


def normalise_kernel(parts_ref, out_ref):
    y, own, odd = place()
    rows = parts_ref.shape[1]
    lane = lanes(rows)
    end = jnp.where(odd, 0, LOOKS - 1)
    own_tile = jnp.where(odd, Y, 0)
    sides = []
    for side in range(2):

        def window(part, base):
            return pltpu.roll(part, (base + 2 * LANES - side * WINDOW) % LANES, 1)

        summed = window(parts_ref[Y - own_tile + Y - 1], base_of(Y - 1, ~odd))
        summed = jnp.where(lane == end, summed, 0.0)
        for i in range(Y):
            base = base_of(i, odd)
            inside = (lane >= base) & (lane < base + WINDOW)
            summed = summed + jnp.where(inside, window(parts_ref[own_tile + i], base), 0.0)
        sides.append(summed)
    column_powers = [summed[16:24] for summed in sides]
    row_power = jnp.where(own == 0, *column_powers)
    row = lax.broadcasted_iota(jnp.int32, row_power.shape, 0)
    row_power = jnp.where(row // 2 == y, row_power, 0.0)
    row_power = row_power + pltpu.roll(row_power, 4, 0)
    row_power = row_power + pltpu.roll(row_power, 2, 0)
    for side in range(2):
        scale = lax.rsqrt((row_power + EPSILON) * (column_powers[side] + EPSILON))
        for k in range(2):
            values = sides[side][8 * k : 8 * k + 8] * scale
            for j in range(Y):
                out_ref[2 * j + side, k] = values[2 * j : 2 * j + 2]


def call(kernel, out_shape, operands, scratch=(), flops=0):
    return pl.pallas_call(
        kernel,
        out_shape=out_shape,
        in_specs=[VMEM] * len(operands),
        out_specs=jax.tree.map(lambda _: VMEM, out_shape),
        scratch_shapes=list(scratch),
        compiler_params=pltpu.CompilerParams(vmem_limit_bytes=VMEM_LIMIT),
        cost_estimate=pl.CostEstimate(flops=flops, bytes_accessed=1 << 20, transcendentals=0),
    )(*operands)


def looks(kernel, out_shape, operands, fields):
    rows, samples = 2 * fields * LINES, BLOCKS * LANES
    scratch = [pltpu.VMEM((rows, samples), bf16), pltpu.VMEM((rows, LANES), f32)]
    return call(kernel, out_shape, operands, scratch, flops=2 * rows * samples * LANES)


def local(stack):
    tiles = lax.axis_size("rng")
    axes = ("pair", "rng")

    def device(y, h, n):
        return (2 * y + h) * tiles + n

    def across(ys, cores=(0, 1)):
        pairs = [(y, h, n) for y in ys for h in range(2) for n in range(tiles) if n % 2 in cores]
        return [(device(y, h, n), device(y, 1 - h, n)) for y, h, n in pairs]

    swap = []
    for h in range(2):
        for n in range(1, tiles - 1, 2):
            swap += [(device(0, h, n), device(0, h, n + 1)), (device(0, h, n + 1), device(0, h, n))]
    chips = [[device(y, h, n + c) for c in range(2) for y in range(Y)] for h in range(2) for n in range(0, tiles, 2)]

    chunks = call(cut_kernel, jax.ShapeDtypeStruct((Y, 2, BLOCKS, LINES, LANES), bf16), (stack,))
    group = lax.all_to_all(chunks, "pair", 0, 0, axis_index_groups=GROUPS)
    edge = call(edge_kernel, jax.ShapeDtypeStruct((2, LINES, LANES), bf16), (group,))
    halo = lax.ppermute(edge, axes, swap)
    others = [lax.ppermute(group, axes, across((1, 2, 3), (core,))) for core in range(2)]
    joined = call(join_kernel, jax.ShapeDtypeStruct((2 * Y * SHARES[0] + 2, LINES, LANES), bf16), (group, halo))
    joineds = [lax.ppermute(joined, axes, across((0,), (core,))) for core in range(2)]

    shapes = (
        jax.ShapeDtypeStruct((2 * N_INNER, LANES), f32),
        jax.ShapeDtypeStruct((BLOCKS * LANES, LANES), bf16),
    )
    inner, weights = looks(inner_kernel, shapes, (group, halo), N_INNER)
    parts = looks(
        outer_kernel,
        jax.ShapeDtypeStruct((Y, 24, LANES), f32),
        (group, halo, *others, *joineds, weights, inner),
        N_OUTER,
    )
    parts = lax.all_to_all(jnp.concatenate([parts, parts]), axes, 0, 0, axis_index_groups=chips)
    out = call(normalise_kernel, jax.ShapeDtypeStruct((2 * Y, 2, 2, LANES), f32), (parts,))
    return out[None]


def solution(mesh):
    in_specs = (P("pair", None, None, "rng"),)
    out_specs = P("pair", None, None, None, "rng")
    return jax.shard_map(local, mesh=mesh, in_specs=in_specs, out_specs=out_specs, check_vma=False)
```

```python
import jax
import jax.numpy as jnp
from jax import lax
from jax.experimental import pallas as pl
from jax.experimental.pallas import tpu as pltpu
from jax.sharding import PartitionSpec as P

AZ_TAPS = 31
RG_TAPS = 60
AZ_STEP = 8
RG_STEP = 20
LINES = 16
LANES = 128
SLOT = 32
WINDOW = 64
EPSILON = 1e-06
VMEM_LIMIT = 8 << 20

Y = 4
GROUPS = [[0, 2, 4, 6], [1, 3, 5, 7]]
INNER = [(i, j) for i in range(Y) for j in range(i + 1, Y)]
SHARES = (2, 6, 6, 6)
BLOCKS = max(SHARES)
LOOKS = sum(SHARES) * LANES // RG_STEP
N_INNER = Y + 2 * len(INNER)
N_OUTER = Y + 2 * Y * Y

f32 = jnp.float32
bf16 = jnp.bfloat16
VMEM = pl.BlockSpec(memory_space=pltpu.VMEM)


def place():
    pair = lax.axis_index("pair")
    return pair // 2, pair % 2, lax.axis_index("rng") % 2 == 1


def starts():
    return [sum(SHARES[:y]) for y in range(Y)], [sum(SHARES[y + 1 :]) for y in range(Y)]


def start_of(y, odd):
    even_tile, odd_tile = starts()
    return jnp.where(odd, odd_tile[y], even_tile[y])


def base_of(y, odd):
    even_tile, odd_tile = ([start * LANES // RG_STEP - 1 for start in tile] for tile in starts())
    return jnp.where(odd, odd_tile[y], even_tile[y])


def pick(y, values):
    out = jnp.int32(values[0])
    for i in range(1, Y):
        out = jnp.where(y == i, values[i], out)
    return out


def lanes(rows):
    return lax.broadcasted_iota(jnp.int32, (rows, LANES), 1)


def azimuth_weights():
    line = lax.broadcasted_iota(jnp.int32, (LINES, LANES), 0)
    weights = []
    for look in range(LINES // AZ_STEP):
        offset = line - (AZ_STEP * look + (AZ_STEP - AZ_TAPS) // 2)
        centred = (offset.astype(f32) - (AZ_TAPS - 1) / 2.0) / (AZ_TAPS / 4.0)
        inside = (offset >= 0) & (offset < AZ_TAPS)
        weights.append(jnp.where(inside, jnp.exp(-0.5 * centred * centred), 0.0))
    return weights


def range_weights(y, odd):
    shape = (BLOCKS * LANES, LANES)
    row = lax.broadcasted_iota(jnp.int32, shape, 0)
    column = lax.broadcasted_iota(jnp.int32, shape, 1) % WINDOW
    look = column + pick(y, [base_of(i, odd) for i in range(Y)])
    start = pick(y, [start_of(i, odd) for i in range(Y)])
    count = pick(y, SHARES) * LANES
    halo = row - (BLOCKS - 1) * LANES
    beyond = halo + jnp.where(odd, sum(SHARES) * LANES, -RG_STEP)
    own = row < count
    sample = jnp.where(own, start * LANES + row, beyond)
    tap = sample - RG_STEP * (look - 1)
    centred = (tap.astype(f32) - (RG_TAPS - 1) / 2.0) / (RG_TAPS / 4.0)
    inside = (tap >= 0) & (tap < RG_TAPS) & (own | ((y == 0) & (halo >= 0) & (halo < RG_STEP)))
    return jnp.where(inside, 2.0 * jnp.exp(-0.5 * centred * centred), 0.0)


def cut_kernel(stack_ref, out_ref):
    _, _, odd = place()
    for y in range(Y):
        start = start_of(y, odd)
        for part in range(2):
            for t in range(BLOCKS):
                if t < SHARES[y]:
                    at = pl.multiple_of((start + t) * LANES, LANES)
                    out_ref[y, part, t] = stack_ref[0, part, :, pl.ds(at, LANES)]
                else:
                    out_ref[y, part, t] = jnp.zeros((LINES, LANES), bf16)


def edge_kernel(group_ref, edge_ref):
    _, _, odd = place()
    for part in range(2):
        packed = jnp.zeros((LINES, LANES), f32)
        for i in range(Y):
            first = group_ref[i, part, 0].astype(f32)
            last = group_ref[i, part, SHARES[0] - 1].astype(f32)
            edge = jnp.where(odd, pltpu.roll(last, RG_STEP, 1), first)
            edge = jnp.where(lanes(LINES) < RG_STEP, edge, 0.0)
            packed = packed + (pltpu.roll(edge, SLOT * i, 1) if i else edge)
        edge_ref[part] = packed.astype(bf16)


def join_kernel(group_ref, halo_ref, out_ref):
    share = SHARES[0]
    for i in range(Y):
        for part in range(2):
            for t in range(share):
                out_ref[(2 * i + part) * share + t] = group_ref[i, part, t]
    for part in range(2):
        out_ref[2 * Y * share + part] = halo_ref[part]


def unpack(packed, i):
    rolled = pltpu.roll(packed, LANES - SLOT * i, 1) if i else packed
    return jnp.where(lanes(LINES) < RG_STEP, rolled, 0.0)


def dates_at(refs, t, halos, joined_refs=()):
    def one(i, part):
        value = sum(ref[i, part, t].astype(f32) for ref in refs)
        if t < SHARES[0]:
            value = value + sum(ref[(2 * i + part) * SHARES[0] + t].astype(f32) for ref in joined_refs)
        if t == BLOCKS - 1:
            value = value + unpack(halos[part], i)
        return value

    return [(one(i, 0), one(i, 1)) for i in range(Y)]


def power(date):
    x, y = date
    return ((0.5 * x) * x + (0.5 * y) * y,)


def cross(row, column):
    hx, hy = 0.5 * row[0], 0.5 * row[1]
    x, y = column
    return hx * x + hy * y, hy * x - hx * y


def put(x_ref, fields, t, values):
    at = t % 2 * LANES
    for field, value in enumerate(values):
        high = value.astype(bf16)
        low = (value - high.astype(f32)).astype(bf16)
        x_ref[t // 2, field * LINES : (field + 1) * LINES, at : at + LANES] = high
        x_ref[t // 2, (fields + field) * LINES : (fields + field + 1) * LINES, at : at + LANES] = low


def contract(x_ref, weight_ref, d_ref, t):
    if t % 2 == 1:
        rows = slice((t - 1) * LANES, (t + 1) * LANES)
        part = jnp.dot(x_ref[t // 2], weight_ref[rows, :], preferred_element_type=f32)
        d_ref[...] = part if t == 1 else d_ref[...] + part


def looks_of(d_ref, fields):
    azimuth = azimuth_weights()
    for field in range(fields):
        high = d_ref[field * LINES : (field + 1) * LINES, :]
        low = d_ref[(fields + field) * LINES : (fields + field + 1) * LINES, :]
        both = high + low
        summed = both + pltpu.roll(both, WINDOW, 1)
        for a, weight in enumerate(azimuth):
            yield field, a, jnp.sum(summed * weight, axis=0, keepdims=True)


def inner_kernel(group_ref, halo_ref, out_ref, weight_ref, x_ref, d_ref):
    y, _, odd = place()
    weights = range_weights(y, odd)
    high = weights.astype(bf16)
    low = (weights - high.astype(f32)).astype(bf16)
    column = lax.broadcasted_iota(jnp.int32, weights.shape, 1)
    weight_ref[...] = jnp.where(column < WINDOW, high.astype(f32), low.astype(f32)).astype(bf16)
    halos = [halo_ref[part].astype(f32) for part in range(2)]
    for t in range(BLOCKS):
        group = dates_at([group_ref], t, halos)
        fields = [power(d) for d in group] + [cross(group[i], group[j]) for i, j in INNER]
        put(x_ref, N_INNER, t, [value for field in fields for value in field])
        contract(x_ref, weight_ref, d_ref, t)
    for field, a, row in looks_of(d_ref, N_INNER):
        out_ref[2 * field + a : 2 * field + a + 1, :] = row


def outer_kernel(group_ref, halo_ref, even_ref, odd_ref, *refs):
    *joined_refs, weight_ref, inner_ref, out_ref, x_ref, d_ref = refs
    _, own, _ = place()
    halos = [halo_ref[part].astype(f32) for part in range(2)]
    other_halos = [sum(ref[2 * Y * SHARES[0] + part].astype(f32) for ref in joined_refs) for part in range(2)]
    for t in range(BLOCKS):
        group, other = dates_at([group_ref], t, halos), dates_at([even_ref, odd_ref], t, other_halos, joined_refs)
        fields = [power(d) for d in other] + [cross(i, j) for i in group for j in other]
        put(x_ref, N_OUTER, t, [value for field in fields for value in field])
        contract(x_ref, weight_ref, d_ref, t)

    first = lanes(1) < WINDOW
    mine = (first & (own == 0)) | (~first & (own == 1))

    def inner(field, a):
        return inner_ref[2 * field + a : 2 * field + a + 1, :]

    def inner_part(i, j, part, a):
        if i == j:
            return inner(i, a) if part == 0 else jnp.zeros((1, LANES), f32)
        field = Y + 2 * INNER.index((min(i, j), max(i, j))) + part
        return -inner(field, a) if part == 1 and i > j else inner(field, a)

    for field, a, row in looks_of(d_ref, N_OUTER):
        if field < Y:
            at = 16 + 2 * field + a
            row = jnp.where(mine, inner(field, a), row)
            for i in range(Y):
                out_ref[i, at : at + 1, :] = row
        else:
            i, j = divmod((field - Y) // 2, Y)
            part = (field - Y) % 2
            at = 8 * part + 2 * j + a
            out_ref[i, at : at + 1, :] = jnp.where(mine, inner_part(i, j, part, a), row)


def normalise_kernel(parts_ref, out_ref):
    y, own, odd = place()
    rows = parts_ref.shape[1]
    lane = lanes(rows)
    end = jnp.where(odd, 0, LOOKS - 1)
    own_tile = jnp.where(odd, Y, 0)
    sides = []
    for side in range(2):

        def window(part, base):
            return pltpu.roll(part, (base + 2 * LANES - side * WINDOW) % LANES, 1)

        summed = window(parts_ref[Y - own_tile + Y - 1], base_of(Y - 1, ~odd))
        summed = jnp.where(lane == end, summed, 0.0)
        for i in range(Y):
            base = base_of(i, odd)
            inside = (lane >= base) & (lane < base + WINDOW)
            summed = summed + jnp.where(inside, window(parts_ref[own_tile + i], base), 0.0)
        sides.append(summed)
    column_powers = [summed[16:24] for summed in sides]
    row_power = jnp.where(own == 0, *column_powers)
    row = lax.broadcasted_iota(jnp.int32, row_power.shape, 0)
    row_power = jnp.where(row // 2 == y, row_power, 0.0)
    row_power = row_power + pltpu.roll(row_power, 4, 0)
    row_power = row_power + pltpu.roll(row_power, 2, 0)
    for side in range(2):
        scale = lax.rsqrt((row_power + EPSILON) * (column_powers[side] + EPSILON))
        for k in range(2):
            values = sides[side][8 * k : 8 * k + 8] * scale
            for j in range(Y):
                out_ref[2 * j + side, k] = values[2 * j : 2 * j + 2]


def call(kernel, out_shape, operands, scratch=(), flops=0):
    return pl.pallas_call(
        kernel,
        out_shape=out_shape,
        in_specs=[VMEM] * len(operands),
        out_specs=jax.tree.map(lambda _: VMEM, out_shape),
        scratch_shapes=list(scratch),
        compiler_params=pltpu.CompilerParams(vmem_limit_bytes=VMEM_LIMIT),
        cost_estimate=pl.CostEstimate(flops=flops, bytes_accessed=1 << 20, transcendentals=0),
    )(*operands)


def looks(kernel, out_shape, operands, fields):
    rows, samples = 2 * fields * LINES, BLOCKS * LANES
    scratch = [pltpu.VMEM((BLOCKS // 2, rows, 2 * LANES), bf16), pltpu.VMEM((rows, LANES), f32)]
    return call(kernel, out_shape, operands, scratch, flops=2 * rows * samples * LANES)


def local(stack):
    tiles = lax.axis_size("rng")
    axes = ("pair", "rng")

    def device(y, h, n):
        return (2 * y + h) * tiles + n

    def across(ys, cores=(0, 1)):
        pairs = [(y, h, n) for y in ys for h in range(2) for n in range(tiles) if n % 2 in cores]
        return [(device(y, h, n), device(y, 1 - h, n)) for y, h, n in pairs]

    swap = []
    for h in range(2):
        for n in range(1, tiles - 1, 2):
            swap += [(device(0, h, n), device(0, h, n + 1)), (device(0, h, n + 1), device(0, h, n))]
    chips = [[device(y, h, n + c) for c in range(2) for y in range(Y)] for h in range(2) for n in range(0, tiles, 2)]

    chunks = call(cut_kernel, jax.ShapeDtypeStruct((Y, 2, BLOCKS, LINES, LANES), bf16), (stack,))
    group = lax.all_to_all(chunks, "pair", 0, 0, axis_index_groups=GROUPS)
    edge = call(edge_kernel, jax.ShapeDtypeStruct((2, LINES, LANES), bf16), (group,))
    halo = lax.ppermute(edge, axes, swap)
    others = [lax.ppermute(group, axes, across((1, 2, 3), (core,))) for core in range(2)]
    joined = call(join_kernel, jax.ShapeDtypeStruct((2 * Y * SHARES[0] + 2, LINES, LANES), bf16), (group, halo))
    joineds = [lax.ppermute(joined, axes, across((0,), (core,))) for core in range(2)]

    shapes = (
        jax.ShapeDtypeStruct((2 * N_INNER, LANES), f32),
        jax.ShapeDtypeStruct((BLOCKS * LANES, LANES), bf16),
    )
    inner, weights = looks(inner_kernel, shapes, (group, halo), N_INNER)
    parts = looks(
        outer_kernel,
        jax.ShapeDtypeStruct((Y, 24, LANES), f32),
        (group, halo, *others, *joineds, weights, inner),
        N_OUTER,
    )
    parts = lax.all_to_all(jnp.concatenate([parts, parts]), axes, 0, 0, axis_index_groups=chips)
    out = call(normalise_kernel, jax.ShapeDtypeStruct((2 * Y, 2, 2, LANES), f32), (parts,))
    return out[None]


def solution(mesh):
    in_specs = (P("pair", None, None, "rng"),)
    out_specs = P("pair", None, None, None, "rng")
    return jax.shard_map(local, mesh=mesh, in_specs=in_specs, out_specs=out_specs, check_vma=False)
```

```python
import jax
import jax.numpy as jnp
from jax import lax
from jax.experimental import pallas as pl
from jax.experimental.pallas import tpu as pltpu
from jax.sharding import PartitionSpec as P

AZ_TAPS = 31
RG_TAPS = 60
AZ_STEP = 8
RG_STEP = 20
LINES = 16
LANES = 128
SLOT = 32
WINDOW = 64
EPSILON = 1e-06
VMEM_LIMIT = 8 << 20

Y = 4
GROUPS = [[0, 2, 4, 6], [1, 3, 5, 7]]
INNER = [(i, j) for i in range(Y) for j in range(i + 1, Y)]
SHARES = (2, 6, 6, 6)
BLOCKS = max(SHARES)
LOOKS = sum(SHARES) * LANES // RG_STEP
N_INNER = Y + 2 * len(INNER)
N_OUTER = Y + 2 * Y * Y

f32 = jnp.float32
bf16 = jnp.bfloat16
VMEM = pl.BlockSpec(memory_space=pltpu.VMEM)


def place():
    pair = lax.axis_index("pair")
    return pair // 2, pair % 2, lax.axis_index("rng") % 2 == 1


def starts():
    return [sum(SHARES[:y]) for y in range(Y)], [sum(SHARES[y + 1 :]) for y in range(Y)]


def start_of(y, odd):
    even_tile, odd_tile = starts()
    return jnp.where(odd, odd_tile[y], even_tile[y])


def base_of(y, odd):
    even_tile, odd_tile = ([start * LANES // RG_STEP - 1 for start in tile] for tile in starts())
    return jnp.where(odd, odd_tile[y], even_tile[y])


def pick(y, values):
    out = jnp.int32(values[0])
    for i in range(1, Y):
        out = jnp.where(y == i, values[i], out)
    return out


def lanes(rows):
    return lax.broadcasted_iota(jnp.int32, (rows, LANES), 1)


def azimuth_weights():
    line = lax.broadcasted_iota(jnp.int32, (LINES, LANES), 0)
    weights = []
    for look in range(LINES // AZ_STEP):
        offset = line - (AZ_STEP * look + (AZ_STEP - AZ_TAPS) // 2)
        centred = (offset.astype(f32) - (AZ_TAPS - 1) / 2.0) / (AZ_TAPS / 4.0)
        inside = (offset >= 0) & (offset < AZ_TAPS)
        weights.append(jnp.where(inside, jnp.exp(-0.5 * centred * centred), 0.0))
    return weights


def range_weights(y, odd):
    shape = (BLOCKS * LANES, LANES)
    row = lax.broadcasted_iota(jnp.int32, shape, 0)
    column = lax.broadcasted_iota(jnp.int32, shape, 1) % WINDOW
    look = column + pick(y, [base_of(i, odd) for i in range(Y)])
    start = pick(y, [start_of(i, odd) for i in range(Y)])
    count = pick(y, SHARES) * LANES
    halo = row - (BLOCKS - 1) * LANES
    beyond = halo + jnp.where(odd, sum(SHARES) * LANES, -RG_STEP)
    own = row < count
    sample = jnp.where(own, start * LANES + row, beyond)
    tap = sample - RG_STEP * (look - 1)
    centred = (tap.astype(f32) - (RG_TAPS - 1) / 2.0) / (RG_TAPS / 4.0)
    inside = (tap >= 0) & (tap < RG_TAPS) & (own | ((y == 0) & (halo >= 0) & (halo < RG_STEP)))
    return jnp.where(inside, 2.0 * jnp.exp(-0.5 * centred * centred), 0.0)


def cut_kernel(stack_ref, out_ref):
    _, _, odd = place()
    for y in range(Y):
        start = start_of(y, odd)
        for part in range(2):
            for t in range(BLOCKS):
                if t < SHARES[y]:
                    at = pl.multiple_of((start + t) * LANES, LANES)
                    out_ref[y, part, t] = stack_ref[0, part, :, pl.ds(at, LANES)]
                else:
                    out_ref[y, part, t] = jnp.zeros((LINES, LANES), bf16)


def edge_kernel(group_ref, edge_ref):
    _, _, odd = place()
    for part in range(2):
        packed = jnp.zeros((LINES, LANES), f32)
        for i in range(Y):
            first = group_ref[i, part, 0].astype(f32)
            last = group_ref[i, part, SHARES[0] - 1].astype(f32)
            edge = jnp.where(odd, pltpu.roll(last, RG_STEP, 1), first)
            edge = jnp.where(lanes(LINES) < RG_STEP, edge, 0.0)
            packed = packed + (pltpu.roll(edge, SLOT * i, 1) if i else edge)
        edge_ref[part] = packed.astype(bf16)


def join_kernel(group_ref, halo_ref, out_ref):
    share = SHARES[0]
    for i in range(Y):
        for part in range(2):
            for t in range(share):
                out_ref[(2 * i + part) * share + t] = group_ref[i, part, t]
    for part in range(2):
        out_ref[2 * Y * share + part] = halo_ref[part]


def unpack(packed, i):
    rolled = pltpu.roll(packed, LANES - SLOT * i, 1) if i else packed
    return jnp.where(lanes(LINES) < RG_STEP, rolled, 0.0)


def dates_at(refs, t, halos, joined_refs=()):
    def one(i, part):
        value = sum(ref[i, part, t].astype(f32) for ref in refs)
        if t < SHARES[0]:
            value = value + sum(ref[(2 * i + part) * SHARES[0] + t].astype(f32) for ref in joined_refs)
        if t == BLOCKS - 1:
            value = value + unpack(halos[part], i)
        return value

    return [(one(i, 0), one(i, 1)) for i in range(Y)]


def power(date):
    x, y = date
    return ((0.5 * x) * x + (0.5 * y) * y,)


def cross(row, column):
    hx, hy = 0.5 * row[0], 0.5 * row[1]
    x, y = column
    return hx * x + hy * y, hy * x - hx * y


def put(x_ref, fields, t, values):
    at = t * LANES
    for field, value in enumerate(values):
        high = value.astype(bf16)
        low = (value - high.astype(f32)).astype(bf16)
        x_ref[field * LINES : (field + 1) * LINES, at : at + LANES] = high
        x_ref[(fields + field) * LINES : (fields + field + 1) * LINES, at : at + LANES] = low


def looks_of(x_ref, weights, d_ref, fields):
    d_ref[...] = jnp.dot(x_ref[...], weights, preferred_element_type=f32)
    azimuth = azimuth_weights()
    for field in range(fields):
        high = d_ref[field * LINES : (field + 1) * LINES, :]
        low = d_ref[(fields + field) * LINES : (fields + field + 1) * LINES, :]
        both = high + low
        summed = both + pltpu.roll(both, WINDOW, 1)
        for a, weight in enumerate(azimuth):
            yield field, a, jnp.sum(summed * weight, axis=0, keepdims=True)


def inner_kernel(group_ref, halo_ref, out_ref, weight_ref, x_ref, d_ref):
    y, _, odd = place()
    weights = range_weights(y, odd)
    high = weights.astype(bf16)
    low = (weights - high.astype(f32)).astype(bf16)
    column = lax.broadcasted_iota(jnp.int32, weights.shape, 1)
    weight_ref[...] = jnp.where(column < WINDOW, high.astype(f32), low.astype(f32)).astype(bf16)
    halos = [halo_ref[part].astype(f32) for part in range(2)]
    for t in range(BLOCKS):
        group = dates_at([group_ref], t, halos)
        fields = [power(d) for d in group] + [cross(group[i], group[j]) for i, j in INNER]
        put(x_ref, N_INNER, t, [value for field in fields for value in field])
    for field, a, row in looks_of(x_ref, weight_ref[...], d_ref, N_INNER):
        out_ref[2 * field + a : 2 * field + a + 1, :] = row


def outer_kernel(group_ref, halo_ref, even_ref, odd_ref, *refs):
    *joined_refs, weight_ref, inner_ref, out_ref, x_ref, d_ref = refs
    _, own, _ = place()
    halos = [halo_ref[part].astype(f32) for part in range(2)]
    other_halos = [sum(ref[2 * Y * SHARES[0] + part].astype(f32) for ref in joined_refs) for part in range(2)]
    for t in range(BLOCKS):
        group, other = dates_at([group_ref], t, halos), dates_at([even_ref, odd_ref], t, other_halos, joined_refs)
        fields = [power(d) for d in other] + [cross(i, j) for i in group for j in other]
        put(x_ref, N_OUTER, t, [value for field in fields for value in field])

    first = lanes(1) < WINDOW
    mine = (first & (own == 0)) | (~first & (own == 1))

    def inner(field, a):
        return inner_ref[2 * field + a : 2 * field + a + 1, :]

    def inner_part(i, j, part, a):
        if i == j:
            return inner(i, a) if part == 0 else jnp.zeros((1, LANES), f32)
        field = Y + 2 * INNER.index((min(i, j), max(i, j))) + part
        return -inner(field, a) if part == 1 and i > j else inner(field, a)

    for field, a, row in looks_of(x_ref, weight_ref[...], d_ref, N_OUTER):
        if field < Y:
            at = 16 + 2 * field + a
            row = jnp.where(mine, inner(field, a), row)
            for i in range(Y):
                out_ref[i, at : at + 1, :] = row
        else:
            i, j = divmod((field - Y) // 2, Y)
            part = (field - Y) % 2
            at = 8 * part + 2 * j + a
            out_ref[i, at : at + 1, :] = jnp.where(mine, inner_part(i, j, part, a), row)


def normalise_kernel(parts_ref, out_ref):
    y, own, odd = place()
    rows = parts_ref.shape[1]
    lane = lanes(rows)
    end = jnp.where(odd, 0, LOOKS - 1)
    own_tile = jnp.where(odd, Y, 0)
    sides = []
    for side in range(2):

        def window(part, base):
            return pltpu.roll(part, (base + 2 * LANES - side * WINDOW) % LANES, 1)

        summed = window(parts_ref[Y - own_tile + Y - 1], base_of(Y - 1, ~odd))
        summed = jnp.where(lane == end, summed, 0.0)
        for i in range(Y):
            base = base_of(i, odd)
            inside = (lane >= base) & (lane < base + WINDOW)
            summed = summed + jnp.where(inside, window(parts_ref[own_tile + i], base), 0.0)
        sides.append(summed)
    column_powers = [summed[16:24] for summed in sides]
    row_power = jnp.where(own == 0, *column_powers)
    row = lax.broadcasted_iota(jnp.int32, row_power.shape, 0)
    row_power = jnp.where(row // 2 == y, row_power, 0.0)
    row_power = row_power + pltpu.roll(row_power, 4, 0)
    row_power = row_power + pltpu.roll(row_power, 2, 0)
    for side in range(2):
        scale = lax.rsqrt((row_power + EPSILON) * (column_powers[side] + EPSILON))
        for k in range(2):
            values = sides[side][8 * k : 8 * k + 8] * scale
            for j in range(Y):
                out_ref[2 * j + side, k] = values[2 * j : 2 * j + 2]


def call(kernel, out_shape, operands, scratch=(), flops=0):
    return pl.pallas_call(
        kernel,
        out_shape=out_shape,
        in_specs=[VMEM] * len(operands),
        out_specs=jax.tree.map(lambda _: VMEM, out_shape),
        scratch_shapes=list(scratch),
        compiler_params=pltpu.CompilerParams(vmem_limit_bytes=VMEM_LIMIT),
        cost_estimate=pl.CostEstimate(flops=flops, bytes_accessed=1 << 20, transcendentals=0),
    )(*operands)


def looks(kernel, out_shape, operands, fields):
    rows, samples = 2 * fields * LINES, BLOCKS * LANES
    scratch = [pltpu.VMEM((rows, samples), bf16), pltpu.VMEM((rows, LANES), f32)]
    return call(kernel, out_shape, operands, scratch, flops=2 * rows * samples * LANES)


def local(stack):
    tiles = lax.axis_size("rng")
    axes = ("pair", "rng")

    def device(y, h, n):
        return (2 * y + h) * tiles + n

    def across(ys, cores=(0, 1)):
        pairs = [(y, h, n) for y in ys for h in range(2) for n in range(tiles) if n % 2 in cores]
        return [(device(y, h, n), device(y, 1 - h, n)) for y, h, n in pairs]

    swap = []
    for h in range(2):
        for n in range(1, tiles - 1, 2):
            swap += [(device(0, h, n), device(0, h, n + 1)), (device(0, h, n + 1), device(0, h, n))]
    chips = [[device(y, h, n + c) for c in range(2) for y in range(Y)] for h in range(2) for n in range(0, tiles, 2)]

    chunks = call(cut_kernel, jax.ShapeDtypeStruct((Y, 2, BLOCKS, LINES, LANES), bf16), (stack,))
    group = lax.all_to_all(chunks, "pair", 0, 0, axis_index_groups=GROUPS)
    edge = call(edge_kernel, jax.ShapeDtypeStruct((2, LINES, LANES), bf16), (group,))
    halo = lax.ppermute(edge, axes, swap)
    others = [lax.ppermute(group, axes, across((1, 2, 3), (core,))) for core in range(2)]
    joined = call(join_kernel, jax.ShapeDtypeStruct((2 * Y * SHARES[0] + 2, LINES, LANES), bf16), (group, halo))
    joineds = [lax.ppermute(joined, axes, across((0,), (core,))) for core in (1, 0)]

    shapes = (
        jax.ShapeDtypeStruct((2 * N_INNER, LANES), f32),
        jax.ShapeDtypeStruct((BLOCKS * LANES, LANES), bf16),
    )
    inner, weights = looks(inner_kernel, shapes, (group, halo), N_INNER)
    parts = looks(
        outer_kernel,
        jax.ShapeDtypeStruct((Y, 24, LANES), f32),
        (group, halo, *others, *joineds, weights, inner),
        N_OUTER,
    )
    parts = lax.all_to_all(jnp.concatenate([parts, parts]), axes, 0, 0, axis_index_groups=chips)
    out = call(normalise_kernel, jax.ShapeDtypeStruct((2 * Y, 2, 2, LANES), f32), (parts,))
    return out[None]


def solution(mesh):
    in_specs = (P("pair", None, None, "rng"),)
    out_specs = P("pair", None, None, None, "rng")
    return jax.shard_map(local, mesh=mesh, in_specs=in_specs, out_specs=out_specs, check_vma=False)
```

```python
import jax
import jax.numpy as jnp
from jax import lax
from jax.experimental import pallas as pl
from jax.experimental.pallas import tpu as pltpu
from jax.sharding import PartitionSpec as P

AZ_TAPS = 31
RG_TAPS = 60
AZ_STEP = 8
RG_STEP = 20
LINES = 16
LANES = 128
SLOT = 32
WINDOW = 64
EPSILON = 1e-06
VMEM_LIMIT = 8 << 20

Y = 4
GROUPS = [[0, 2, 4, 6], [1, 3, 5, 7]]
INNER = [(i, j) for i in range(Y) for j in range(i + 1, Y)]
SHARES = (2, 6, 6, 6)
BLOCKS = max(SHARES)
LOOKS = sum(SHARES) * LANES // RG_STEP
N_INNER = Y + 2 * len(INNER)
N_OUTER = Y + 2 * Y * Y

f32 = jnp.float32
bf16 = jnp.bfloat16
VMEM = pl.BlockSpec(memory_space=pltpu.VMEM)


def place():
    pair = lax.axis_index("pair")
    return pair // 2, pair % 2, lax.axis_index("rng") % 2 == 1


def starts():
    return [sum(SHARES[:y]) for y in range(Y)], [sum(SHARES[y + 1 :]) for y in range(Y)]


def start_of(y, odd):
    even_tile, odd_tile = starts()
    return jnp.where(odd, odd_tile[y], even_tile[y])


def base_of(y, odd):
    even_tile, odd_tile = ([start * LANES // RG_STEP - 1 for start in tile] for tile in starts())
    return jnp.where(odd, odd_tile[y], even_tile[y])


def pick(y, values):
    out = jnp.int32(values[0])
    for i in range(1, Y):
        out = jnp.where(y == i, values[i], out)
    return out


def lanes(rows):
    return lax.broadcasted_iota(jnp.int32, (rows, LANES), 1)


def azimuth_weights():
    line = lax.broadcasted_iota(jnp.int32, (LINES, LANES), 0)
    weights = []
    for look in range(LINES // AZ_STEP):
        offset = line - (AZ_STEP * look + (AZ_STEP - AZ_TAPS) // 2)
        centred = (offset.astype(f32) - (AZ_TAPS - 1) / 2.0) / (AZ_TAPS / 4.0)
        inside = (offset >= 0) & (offset < AZ_TAPS)
        weights.append(jnp.where(inside, jnp.exp(-0.5 * centred * centred), 0.0))
    return weights


def range_weights(y, odd):
    shape = (BLOCKS * LANES, LANES)
    row = lax.broadcasted_iota(jnp.int32, shape, 0)
    column = lax.broadcasted_iota(jnp.int32, shape, 1) % WINDOW
    look = column + pick(y, [base_of(i, odd) for i in range(Y)])
    start = pick(y, [start_of(i, odd) for i in range(Y)])
    count = pick(y, SHARES) * LANES
    halo = row - (BLOCKS - 1) * LANES
    beyond = halo + jnp.where(odd, sum(SHARES) * LANES, -RG_STEP)
    own = row < count
    sample = jnp.where(own, start * LANES + row, beyond)
    tap = sample - RG_STEP * (look - 1)
    centred = (tap.astype(f32) - (RG_TAPS - 1) / 2.0) / (RG_TAPS / 4.0)
    inside = (tap >= 0) & (tap < RG_TAPS) & (own | ((y == 0) & (halo >= 0) & (halo < RG_STEP)))
    return jnp.where(inside, 2.0 * jnp.exp(-0.5 * centred * centred), 0.0)


def cut_kernel(stack_ref, out_ref):
    _, _, odd = place()
    for y in range(Y):
        start = start_of(y, odd)
        for part in range(2):
            for t in range(BLOCKS):
                if t < SHARES[y]:
                    at = pl.multiple_of((start + t) * LANES, LANES)
                    out_ref[y, part, t] = stack_ref[0, part, :, pl.ds(at, LANES)]
                else:
                    out_ref[y, part, t] = jnp.zeros((LINES, LANES), bf16)


def edge_kernel(group_ref, edge_ref):
    _, _, odd = place()
    for part in range(2):
        packed = jnp.zeros((LINES, LANES), f32)
        for i in range(Y):
            first = group_ref[i, part, 0].astype(f32)
            last = group_ref[i, part, SHARES[0] - 1].astype(f32)
            edge = jnp.where(odd, pltpu.roll(last, RG_STEP, 1), first)
            edge = jnp.where(lanes(LINES) < RG_STEP, edge, 0.0)
            packed = packed + (pltpu.roll(edge, SLOT * i, 1) if i else edge)
        edge_ref[part] = packed.astype(bf16)


def join_kernel(group_ref, halo_ref, out_ref):
    share = SHARES[0]
    for i in range(Y):
        for part in range(2):
            for t in range(share):
                out_ref[(2 * i + part) * share + t] = group_ref[i, part, t]
    for part in range(2):
        out_ref[2 * Y * share + part] = halo_ref[part]


def unpack(packed, i):
    rolled = pltpu.roll(packed, LANES - SLOT * i, 1) if i else packed
    return jnp.where(lanes(LINES) < RG_STEP, rolled, 0.0)


def dates_at(refs, t, halos, joined_refs=()):
    def one(i, part):
        value = sum(ref[i, part, t].astype(f32) for ref in refs)
        if t < SHARES[0]:
            value = value + sum(ref[(2 * i + part) * SHARES[0] + t].astype(f32) for ref in joined_refs)
        if t == BLOCKS - 1:
            value = value + unpack(halos[part], i)
        return value

    return [(one(i, 0), one(i, 1)) for i in range(Y)]


def power(date):
    x, y = date
    return ((0.5 * x) * x + (0.5 * y) * y,)


def cross(row, column):
    hx, hy = 0.5 * row[0], 0.5 * row[1]
    x, y = column
    return hx * x + hy * y, hy * x - hx * y


def put(x_ref, fields, t, values):
    at = t * LANES
    for field, value in enumerate(values):
        high = value.astype(bf16)
        low = (value - high.astype(f32)).astype(bf16)
        x_ref[field * LINES : (field + 1) * LINES, at : at + LANES] = high
        x_ref[(fields + field) * LINES : (fields + field + 1) * LINES, at : at + LANES] = low


def looks_of(x_ref, weights, d_ref, fields):
    d_ref[...] = jnp.dot(x_ref[...], weights, preferred_element_type=f32)
    azimuth = azimuth_weights()
    for field in range(fields):
        high = d_ref[field * LINES : (field + 1) * LINES, :]
        low = d_ref[(fields + field) * LINES : (fields + field + 1) * LINES, :]
        both = high + low
        summed = both + pltpu.roll(both, WINDOW, 1)
        for a, weight in enumerate(azimuth):
            yield field, a, jnp.sum(summed * weight, axis=0, keepdims=True)


def inner_kernel(group_ref, halo_ref, out_ref, weight_ref, x_ref, d_ref):
    y, _, odd = place()
    weights = range_weights(y, odd)
    high = weights.astype(bf16)
    low = (weights - high.astype(f32)).astype(bf16)
    column = lax.broadcasted_iota(jnp.int32, weights.shape, 1)
    weight_ref[...] = jnp.where(column < WINDOW, high.astype(f32), low.astype(f32)).astype(bf16)
    halos = [halo_ref[part].astype(f32) for part in range(2)]
    for t in range(BLOCKS):
        group = dates_at([group_ref], t, halos)
        fields = [power(d) for d in group] + [cross(group[i], group[j]) for i, j in INNER]
        put(x_ref, N_INNER, t, [value for field in fields for value in field])
    for field, a, row in looks_of(x_ref, weight_ref[...], d_ref, N_INNER):
        out_ref[2 * field + a : 2 * field + a + 1, :] = row


def outer_kernel(group_ref, halo_ref, even_ref, odd_ref, *refs):
    *joined_refs, weight_ref, inner_ref, out_ref, x_ref, d_ref = refs
    _, own, _ = place()
    halos = [halo_ref[part].astype(f32) for part in range(2)]
    other_halos = [sum(ref[2 * Y * SHARES[0] + part].astype(f32) for ref in joined_refs) for part in range(2)]
    for t in range(BLOCKS):
        group, other = dates_at([group_ref], t, halos), dates_at([even_ref, odd_ref], t, other_halos, joined_refs)
        fields = [power(d) for d in other] + [cross(i, j) for i in group for j in other]
        put(x_ref, N_OUTER, t, [value for field in fields for value in field])

    first = lanes(1) < WINDOW
    mine = (first & (own == 0)) | (~first & (own == 1))

    def inner(field, a):
        return inner_ref[2 * field + a : 2 * field + a + 1, :]

    def inner_part(i, j, part, a):
        if i == j:
            return inner(i, a) if part == 0 else jnp.zeros((1, LANES), f32)
        field = Y + 2 * INNER.index((min(i, j), max(i, j))) + part
        return -inner(field, a) if part == 1 and i > j else inner(field, a)

    for field, a, row in looks_of(x_ref, weight_ref[...], d_ref, N_OUTER):
        if field < Y:
            at = 16 + 2 * field + a
            row = jnp.where(mine, inner(field, a), row)
            for i in range(Y):
                out_ref[i, at : at + 1, :] = row
        else:
            i, j = divmod((field - Y) // 2, Y)
            part = (field - Y) % 2
            at = 8 * part + 2 * j + a
            out_ref[i, at : at + 1, :] = jnp.where(mine, inner_part(i, j, part, a), row)


def normalise_kernel(parts_ref, out_ref):
    y, own, odd = place()
    rows = parts_ref.shape[1]
    lane = lanes(rows)
    end = jnp.where(odd, 0, LOOKS - 1)
    core = jnp.where(odd, 1, 0)
    sides = []
    for side in range(2):

        def window(part, base):
            return pltpu.roll(part, (base + 2 * LANES - side * WINDOW) % LANES, 1)

        summed = window(parts_ref[2 * (Y - 1) + 1 - core], base_of(Y - 1, ~odd))
        summed = jnp.where(lane == end, summed, 0.0)
        for i in range(Y):
            base = base_of(i, odd)
            inside = (lane >= base) & (lane < base + WINDOW)
            summed = summed + jnp.where(inside, window(parts_ref[2 * i + core], base), 0.0)
        sides.append(summed)
    column_powers = [summed[16:24] for summed in sides]
    row_power = jnp.where(own == 0, *column_powers)
    row = lax.broadcasted_iota(jnp.int32, row_power.shape, 0)
    row_power = jnp.where(row // 2 == y, row_power, 0.0)
    row_power = row_power + pltpu.roll(row_power, 4, 0)
    row_power = row_power + pltpu.roll(row_power, 2, 0)
    for side in range(2):
        scale = lax.rsqrt((row_power + EPSILON) * (column_powers[side] + EPSILON))
        for k in range(2):
            values = sides[side][8 * k : 8 * k + 8] * scale
            for j in range(Y):
                out_ref[2 * j + side, k] = values[2 * j : 2 * j + 2]


def call(kernel, out_shape, operands, scratch=(), flops=0):
    return pl.pallas_call(
        kernel,
        out_shape=out_shape,
        in_specs=[VMEM] * len(operands),
        out_specs=jax.tree.map(lambda _: VMEM, out_shape),
        scratch_shapes=list(scratch),
        compiler_params=pltpu.CompilerParams(vmem_limit_bytes=VMEM_LIMIT),
        cost_estimate=pl.CostEstimate(flops=flops, bytes_accessed=1 << 20, transcendentals=0),
    )(*operands)


def looks(kernel, out_shape, operands, fields):
    rows, samples = 2 * fields * LINES, BLOCKS * LANES
    scratch = [pltpu.VMEM((rows, samples), bf16), pltpu.VMEM((rows, LANES), f32)]
    return call(kernel, out_shape, operands, scratch, flops=2 * rows * samples * LANES)


def local(stack):
    tiles = lax.axis_size("rng")
    axes = ("pair", "rng")

    def device(y, h, n):
        return (2 * y + h) * tiles + n

    def across(ys, cores=(0, 1)):
        pairs = [(y, h, n) for y in ys for h in range(2) for n in range(tiles) if n % 2 in cores]
        return [(device(y, h, n), device(y, 1 - h, n)) for y, h, n in pairs]

    swap = []
    for h in range(2):
        for n in range(1, tiles - 1, 2):
            swap += [(device(0, h, n), device(0, h, n + 1)), (device(0, h, n + 1), device(0, h, n))]
    chips = [[device(y, h, n + c) for y in range(Y) for c in range(2)] for h in range(2) for n in range(0, tiles, 2)]

    chunks = call(cut_kernel, jax.ShapeDtypeStruct((Y, 2, BLOCKS, LINES, LANES), bf16), (stack,))
    group = lax.all_to_all(chunks, "pair", 0, 0, axis_index_groups=GROUPS)
    edge = call(edge_kernel, jax.ShapeDtypeStruct((2, LINES, LANES), bf16), (group,))
    halo = lax.ppermute(edge, axes, swap)
    others = [lax.ppermute(group, axes, across((1, 2, 3), (core,))) for core in range(2)]
    joined = call(join_kernel, jax.ShapeDtypeStruct((2 * Y * SHARES[0] + 2, LINES, LANES), bf16), (group, halo))
    joineds = [lax.ppermute(joined, axes, across((0,), (core,))) for core in range(2)]

    shapes = (
        jax.ShapeDtypeStruct((2 * N_INNER, LANES), f32),
        jax.ShapeDtypeStruct((BLOCKS * LANES, LANES), bf16),
    )
    inner, weights = looks(inner_kernel, shapes, (group, halo), N_INNER)
    parts = looks(
        outer_kernel,
        jax.ShapeDtypeStruct((Y, 24, LANES), f32),
        (group, halo, *others, *joineds, weights, inner),
        N_OUTER,
    )
    parts = lax.all_to_all(jnp.repeat(parts, 2, axis=0), axes, 0, 0, axis_index_groups=chips)
    out = call(normalise_kernel, jax.ShapeDtypeStruct((2 * Y, 2, 2, LANES), f32), (parts,))
    return out[None]


def solution(mesh):
    in_specs = (P("pair", None, None, "rng"),)
    out_specs = P("pair", None, None, None, "rng")
    return jax.shard_map(local, mesh=mesh, in_specs=in_specs, out_specs=out_specs, check_vma=False)
```
